256 devices in a mesh: depth: 2 (over y_hi), row: 16 (over x, y_lo, core), col: 8 (over z).
Axes of the slice: x: 4, y: 4 (y_hi: 2, y_lo: 2; y = y_hi * 2 + y_lo), z: 8, core: 2. Of those that a mesh axis runs over, the one named last changes fastest.
Arguments:
- volume: bfloat16 [64, 256, 8192], P('depth', 'row', 'col'), may hold values from -6 to 6
- first_weight: bfloat16 [64, 864], replicated, may hold values from -0.21875 to 0.21875
- second_weight: bfloat16 [128, 1728], replicated, may hold values from -0.15625 to 0.15625
- cotangent: bfloat16 [16, 64, 8192], P('depth', 'row', 'col'), may hold values from -0.011962891 to 0.011962891
Outputs:
- first_grad: float32 [64, 864], replicated
- second_grad: float32 [128, 1728], replicated
The draws below stay inside these ranges and needn't reach their ends.
All inputs are finite; a program needn't handle non-finite values.
Results may differ from the reference program's by a relative error of at most 0.0047.
Values may be sent and summed in bfloat16 or wider, within the bound.
A program may use at most 128 MiB of HBM per device.

```python
import jax
import jax.numpy as jnp
from jax import lax

C0 = 32
C1 = 64
C2 = 128
ND = 64
NR = 256
NC = 256


def block_levels(key, dims, pieces, smallest, high):
    gain, own = 1.0, jax.random.fold_in(key, 6)
    for dim, shards_of in pieces:
        steps = jnp.exp(jax.random.uniform(jax.random.fold_in(own, dim), (shards_of,), jnp.float32, smallest / len(pieces), high / len(pieces)))
        gain = gain * jnp.repeat(steps, dims[dim] // shards_of).reshape([-1 if axis == dim else 1 for axis in range(len(dims))])
    return gain


def noise(own_key, dims, deviation, limit, pieces=(), held_as=jnp.bfloat16):
    loudness = block_levels(own_key, dims, pieces, -0.22, 0.18) if pieces else 1.0
    drawn = jax.random.normal(own_key, dims, jnp.float32) * deviation * loudness
    return jnp.minimum(jnp.maximum(drawn, -limit), limit).astype(held_as)


def setup_inputs(seed: int = 0) -> dict:
    seeds = jax.random.split(jax.random.key(seed), 5)
    volume = noise(seeds[0], (ND, NR, NC * C0), 1.0, 6.0, ((0, 2), (1, 16), (2, 8)))
    first_weight = noise(seeds[1], (C1, 27 * C0), (27 * C0) ** -0.5, 0.21875)
    second_weight = noise(seeds[2], (C2, 27 * C1), (27 * C1) ** -0.5, 0.15625)
    cotangent = noise(seeds[3], (ND // 4, NR // 4, NC // 4 * C2), 0.002, 0.011962891, ((0, 2), (1, 16), (2, 8)))
    return {"volume": volume, "first_weight": first_weight, "second_weight": second_weight, "cotangent": cotangent}


def leaky(values):
    return 0.6 * values + 0.4 * (jnp.sqrt(values * values + 1.0) - 1.0)

def leaky_slope(values):
    return 0.6 + 0.4 * values / jnp.sqrt(values * values + 1.0)

def conv_plain(field, weight_mat, in_chan):
    kernel = weight_mat.reshape(weight_mat.shape[0], 3, 3, 3, in_chan).transpose(0, 4, 1, 2, 3)
    result = lax.conv_general_dilated(field[None], kernel, (2, 2, 2), ((1, 0), (1, 0), (1, 0)), dimension_numbers=('NCDHW', 'OIDHW', 'NCDHW'), precision=lax.Precision.HIGHEST)
    return result[0]

def reference(volume, first_weight, second_weight, cotangent):
    volume_f = volume.astype(jnp.float32).reshape(ND, NR, NC, C0).transpose(3, 0, 1, 2)
    upstream = cotangent.astype(jnp.float32).reshape(ND // 4, NR // 4, NC // 4, C2).transpose(3, 0, 1, 2)
    first_f = first_weight.astype(jnp.float32)
    second_f = second_weight.astype(jnp.float32)
    pre_one = conv_plain(volume_f, first_f, C0)
    hidden = lax.optimization_barrier(leaky(pre_one).astype(jnp.bfloat16))
    hidden_f = hidden.astype(jnp.float32)

    def second_section(hidden_in, weight_mat):
        return conv_plain(hidden_in, weight_mat, C1)
    pre_two, pullback_two = jax.vjp(second_section, hidden_f, second_f)
    delta_two = lax.optimization_barrier((upstream * leaky_slope(pre_two)).astype(jnp.bfloat16))
    back_one, second_grad = pullback_two(delta_two.astype(jnp.float32))
    delta_one = lax.optimization_barrier((back_one * leaky_slope(pre_one)).astype(jnp.bfloat16))

    def first_section(weight_mat):
        return conv_plain(volume_f, weight_mat, C0)
    unused_out, pullback_one = jax.vjp(first_section, first_f)
    first_grad = pullback_one(delta_one.astype(jnp.float32))[0]
    return (first_grad, second_grad)
```

```python
import jax
import jax.numpy as jnp
from jax import lax
from jax.experimental import pallas as pl
from jax.experimental.pallas import tpu as pltpu
from jax.sharding import PartitionSpec as P

MESH = pl.DeviceIdType.MESH
F32 = jnp.float32
BF16 = jnp.bfloat16

ROWS = 2304
LINK = BF16


def leaky(values):
    root = lax.rsqrt(values * values + 1.0)
    return 0.6 * values + 0.4 * ((values * values + 1.0) * root - 1.0)


def leaky_slope(values):
    return 0.6 + 0.4 * values * lax.rsqrt(values * values + 1.0)


def dot_nt(lhs, rhs):
    return lax.dot_general(lhs, rhs, (((1,), (1,)), ((), ())), preferred_element_type=F32)


def dot_nn(lhs, rhs):
    return lax.dot_general(lhs, rhs, (((1,), (0,)), ((), ())), preferred_element_type=F32)


def window(ref, *lead):
    low = ref[lead + (pl.ds(0, 8),)].reshape(256, 128)
    high = ref[lead + (pl.ds(1, 8),)].reshape(256, 128)
    return jnp.concatenate([low, high], axis=1)


def make_kernel(n_dep, n_row, n_col):
    n_half = n_row // 2
    n_plane = n_dep * n_half
    chunk = ROWS // (2 * n_plane)
    piece = chunk // n_col

    def kernel(
        vol, w1, w2, cot, g1_out, g2_out,
        s_ref, f_ref, w1f, w2f, w1b, w2b, up,
        sr, f_c, f_r, f_d, f_dc, f_dr, f_drc,
        hs, hx, slope1, h_sc, h_sr, h_sd, h_c, h_r, h_d, h_dr,
        q_ref, dx, d2t, d1t, q_sc, q_sr, q_sd, q_c, q_r, q_d, q_dr,
        acc, half, send1, recv1, send2, recv2, part, send3, recv3, tot, recv4, gath, full,
        halo_send, halo_recv, sum_send, sum_recv,
    ):
        dep, row, col = lax.axis_index("depth"), lax.axis_index("row"), lax.axis_index("col")
        core, line = lax.rem(row, 2), lax.div(row, 2)
        plane = dep * n_half + line

        def plane_dev(index):
            return (lax.div(index, n_half), 2 * lax.rem(index, n_half) + core, col)

        def shifted(step, d, r, c):
            return (
                lax.rem(dep + d * step + n_dep, n_dep),
                lax.rem(row + r * step + n_row, n_row),
                lax.rem(col + c * step + n_col, n_col),
            )

        mate = (dep, row + 1 - 2 * core, col)
        corners = [(d, r, c) for d in (0, 1) for r in (0, 1) for c in (0, 1)][1:]

        barrier = pltpu.get_barrier_semaphore()
        peers = [shifted(s, *e) for e in corners for s in (1, -1)]
        peers.append(mate)
        peers += [plane_dev(lax.rem(plane + s, n_plane)) for s in range(1, n_plane)]
        peers += [(dep, row, lax.rem(col + s, n_col)) for s in range(1, n_col)]
        for peer in peers:
            pl.semaphore_signal(barrier, inc=1, device_id=peer, device_id_type=MESH)

        for rd in range(4):
            for t in range(8):
                s_ref[rd, 1 + t, pl.ds(24, 128), :] = (
                    vol[:, rd, :, pl.ds(128 * t, 128)].astype(F32).reshape(128, 128)
                )
        for t in range(8):
            rows = [s_ref[rd, 1 + t, pl.ds(24 + 15, 8, stride=16), :] for rd in range(4)]
            sr[t] = jnp.concatenate(rows, axis=0).astype(BF16)

        pl.semaphore_wait(barrier, len(peers))

        def halo(phase, kind, src, dst, step):
            index = phase * 7 + kind
            return pltpu.make_async_remote_copy(
                src_ref=src, dst_ref=dst, send_sem=halo_send.at[index], recv_sem=halo_recv.at[index],
                device_id=shifted(step, *corners[kind]), device_id_type=MESH,
            )

        tail = pl.ds(896, 128)
        field_copies = [
            halo(0, 0, vol.at[:, :, :, tail], f_c, 1),
            halo(0, 1, sr, f_r.at[pl.ds(1, 8)], 1),
            halo(0, 2, sr.at[7], f_r.at[0], 1),
            halo(0, 3, vol.at[7, 3], f_d, 1),
            halo(0, 4, vol.at[7, 3, :, tail], f_dc, 1),
            halo(0, 5, vol.at[7, 3], f_dr, 1),
            halo(0, 6, vol.at[7, 3, :, tail], f_drc, 1),
        ]
        for copy in field_copies:
            copy.start()

        w1f[:, pl.ds(768, 128)] = jnp.zeros((64, 128), F32)
        w1f[:, pl.ds(0, 864)] = w1[...].astype(F32)
        w2f[:, pl.ds(1664, 128)] = jnp.zeros((128, 128), F32)
        w2f[:, pl.ds(0, 1728)] = w2[...].astype(F32)
        lane1 = lax.broadcasted_iota(jnp.int32, (64, 256), 1)
        lane2 = lax.broadcasted_iota(jnp.int32, (128, 256), 1)
        for ab in range(9):
            tile, off = divmod(ab * 96, 128)
            if tile == 6:
                band = jnp.concatenate([w1f[:, pl.ds(768, 128)], jnp.zeros((64, 128), F32)], axis=1)
            else:
                band = w1f[:, pl.ds(128 * tile, 256)]
            for kk, start in ((0, 96), (1, 160)):
                moved = pltpu.roll(band, (start - off) % 256, 1)
                keep = (lane1 >= start) & (lane1 < start + 96)
                w1b[ab, pl.ds(64 * kk, 64), :] = jnp.where(keep, moved, 0.0).astype(BF16)
            tile, off = divmod(ab * 192, 128)
            band = w2f[:, pl.ds(128 * tile, 256)]
            moved = band if off == 64 else pltpu.roll(band, 64, 1)
            w2b[ab] = jnp.where(lane2 >= 64, moved, 0.0).astype(BF16)
        for i in range(8):
            line_up = cot[i].astype(F32)
            for k in range(8):
                up[k, pl.ds(4 * i, 4), :] = line_up[:, 128 * k : 128 * (k + 1)]

        def pick_field(t, rd, rr):
            source, start = (3, 8) if rd < 0 else (rd, 24)
            rows = s_ref[source, t, pl.ds(start + rr, 32, stride=4), :]
            f_ref[rd + 1, rr + 1, t] = rows.astype(BF16)

        def local_tile(t, carry):
            for rd in range(4):
                for rr in range(4):
                    pick_field(t, rd, rr)
            return carry

        lax.fori_loop(1, 9, local_tile, 0)

        for copy in field_copies:
            copy.wait()

        first_dep, first_row, first_col = dep == 0, row == 0, col == 0

        def unless(edge, values):
            return jnp.where(edge, 0.0, values.astype(F32))

        for rd in range(4):
            s_ref[rd, 0, pl.ds(24, 128), :] = unless(first_col, f_c[:, rd]).reshape(128, 128)
        for t in range(8):
            s_ref[3, 1 + t, pl.ds(8, 16), :] = unless(first_dep, f_d[:, pl.ds(128 * t, 128)])
        s_ref[3, 0, pl.ds(8, 16), :] = unless(first_dep | first_col, f_dc[...])
        for rd in range(4):
            for rr in range(4):
                pick_field(0, rd, rr)

        def above_tile(t, carry):
            for rr in range(4):
                pick_field(t, -1, rr)
            return carry

        lax.fori_loop(0, 9, above_tile, 0)

        def row_tile(t, carry):
            block = unless(first_row | (first_col & (t == 0)), f_r[t])
            for rd in range(4):
                s_ref[rd, t, pl.ds(23, 8, stride=16), :] = block[8 * rd : 8 * rd + 8]
            return carry

        lax.fori_loop(0, 9, row_tile, 0)
        for t in range(9):
            block = f_drc[...] if t == 0 else f_dr[:, pl.ds(128 * (t - 1), 128)]
            edge = first_dep | first_row
            edge = edge | first_col if t == 0 else edge
            s_ref[3, t, pl.ds(7, 1), :] = unless(edge, block)[15:16]

        def behind_tile(t, carry):
            for rd in range(-1, 4):
                pick_field(t, rd, -1)
            return carry

        lax.fori_loop(0, 9, behind_tile, 0)

        for pd in range(2):
            for pr in range(2):
                pre = jnp.zeros((256, 128), F32)
                for ab in range(9):
                    a, b = divmod(ab, 3)
                    pre += dot_nt(window(f_ref, 2 * pd + a, 2 * pr + b), w1b[ab])
                slope1[pd, pr] = leaky_slope(pre)
                hid = leaky(pre).reshape(8, 32, 128)
                hs[pd, pr, pl.ds(1, 8), pl.ds(8, 32), :] = hid
                h_sc[2 * pd + pr] = hid[7].astype(BF16)
        for t in range(8):
            rows = [hs[pd, 1, 1 + t, pl.ds(11, 8, stride=4), :] for pd in range(2)]
            h_sr[t] = jnp.concatenate(rows, axis=0).astype(BF16)
            rows = [hs[1, pr, 1 + t, pl.ds(32, 8), :] for pr in range(2)]
            h_sd[t] = jnp.concatenate(rows, axis=0).astype(BF16)
        hidden_copies = [
            halo(1, 0, h_sc, h_c, 1),
            halo(1, 1, h_sr, h_r.at[pl.ds(1, 8)], 1),
            halo(1, 2, h_sr.at[7], h_r.at[0], 1),
            halo(1, 3, h_sd, h_d.at[pl.ds(1, 8)], 1),
            halo(1, 4, h_sd.at[7], h_d.at[0], 1),
            halo(1, 5, h_sd, h_dr.at[pl.ds(1, 8)], 1),
            halo(1, 6, h_sd.at[7], h_dr.at[0], 1),
        ]
        for copy in hidden_copies:
            copy.start()
        for copy in hidden_copies:
            copy.wait()
        for pd in range(2):
            for pr in range(2):
                hs[pd, pr, 0, pl.ds(8, 32), :] = unless(first_col, h_c[2 * pd + pr])
        for t in range(9):
            edge = first_dep | first_col if t == 0 else first_dep
            block = unless(edge, h_d[t])
            for pr in range(2):
                hs[1, pr, t, pl.ds(4, 4), :] = block[8 * pr + 4 : 8 * pr + 8]

        def pick_hidden(a, b, pd, pr, start):
            hx[3 * a + b] = hs[pd, pr, :, pl.ds(start, 32), :].astype(BF16)

        for pr in range(2):
            pick_hidden(0, 1 + pr, 1, pr, 4)
            pick_hidden(1, 1 + pr, 0, pr, 8)
            pick_hidden(2, 1 + pr, 1, pr, 8)
        for t in range(9):
            edge = first_row | first_col if t == 0 else first_row
            block = unless(edge, h_r[t])
            for pd in range(2):
                hs[pd, 1, t, pl.ds(7, 8, stride=4), :] = block[8 * pd : 8 * pd + 8]
            block = unless(edge | first_dep, h_dr[t])
            hs[1, 1, t, pl.ds(3, 1), :] = block[15:16]
        pick_hidden(0, 0, 1, 1, 3)
        pick_hidden(1, 0, 0, 1, 7)
        pick_hidden(2, 0, 1, 1, 7)

        pre = jnp.zeros((256, 128), F32)
        for ab in range(9):
            pre += dot_nt(window(hx, ab), w2b[ab])
        delta2 = up[...].reshape(256, 128) * leaky_slope(pre)
        q_ref[pl.ds(0, 8), pl.ds(0, 32), :] = delta2.reshape(8, 32, 128)
        q_sc[...] = delta2[:32].astype(BF16)
        for t in range(8):
            q_sr[t] = q_ref[t, pl.ds(0, 8, stride=4), :]
            q_sd[t] = q_ref[t, pl.ds(0, 8), :]
        delta_copies = [
            halo(2, 0, q_sc, q_c, -1),
            halo(2, 1, q_sr, q_r.at[pl.ds(0, 8)], -1),
            halo(2, 2, q_sr.at[0], q_r.at[8], -1),
            halo(2, 3, q_sd, q_d.at[pl.ds(0, 8)], -1),
            halo(2, 4, q_sd.at[0], q_d.at[8], -1),
            halo(2, 5, q_sd, q_dr.at[pl.ds(0, 8)], -1),
            halo(2, 6, q_sd.at[0], q_dr.at[8], -1),
        ]
        for copy in delta_copies:
            copy.start()

        d2t[...] = delta2.T.astype(BF16)
        lane = lax.broadcasted_iota(jnp.int32, (128, 128), 1)
        held = None
        for ab in range(9):
            grad = dot_nn(d2t[...], window(hx, ab))
            left, right = grad[:, :128], grad[:, 128:]
            tile = 3 * (ab // 2)
            if ab % 2 == 0:
                acc[pl.ds(128 * tile, 128), :] = pltpu.roll(jnp.where(lane >= 64, left, right), 64, 1)
                held = pltpu.roll(right, 64, 1)
            else:
                acc[pl.ds(128 * tile + 128, 128), :] = jnp.where(lane < 64, held, left)
                acc[pl.ds(128 * tile + 256, 128), :] = right
        acc[pl.ds(128 * 13, 128), :] = held

        for copy in delta_copies:
            copy.wait()
        last_dep, last_row, last_col = dep == n_dep - 1, row == n_row - 1, col == n_col - 1
        q_ref[8, pl.ds(0, 32), :] = unless(last_col, q_c[...])
        for t in range(9):
            edge = last_dep | last_col if t == 8 else last_dep
            q_ref[t, pl.ds(32, 4), :] = unless(edge, q_d[t])[:4]
        dx[0] = q_ref[:, pl.ds(0, 32), :].astype(BF16)
        dx[2] = q_ref[:, pl.ds(4, 32), :].astype(BF16)
        for t in range(9):
            edge = last_row | last_col if t == 8 else last_row
            q_ref[t, pl.ds(4, 8, stride=4), :] = unless(edge, q_r[t])
            q_ref[t, pl.ds(36, 1), :] = unless(edge | last_dep, q_dr[t])[:1]
        dx[1] = q_ref[:, pl.ds(1, 32), :].astype(BF16)
        dx[3] = q_ref[:, pl.ds(5, 32), :].astype(BF16)

        taps = (((1, 0),), ((2, 0), (0, 1)))
        for pd in range(2):
            for pr in range(2):
                back = jnp.zeros((256, 128), F32)
                for a, od in taps[pd]:
                    for b, o_r in taps[pr]:
                        band = w2b[3 * a + b]
                        band = jnp.concatenate([band[:, 128:], band[:, :128]], axis=0)
                        back += dot_nn(window(dx, 2 * od + o_r), band)
                delta1 = back * slope1[pd, pr]
                d1t[:, pl.ds(512 * pd + 256 * pr, 256)] = delta1.T.astype(BF16)

        lane = lax.broadcasted_iota(jnp.int32, (64, 256), 1)
        tiles = [jnp.zeros((64, 128), F32) for _ in range(8)]
        for ab in range(9):
            a, b = divmod(ab, 3)
            grad = jnp.zeros((128, 256), F32)
            for pd in range(2):
                for pr in range(2):
                    grad += dot_nn(
                        d1t[:, pl.ds(512 * pd + 256 * pr, 256)], window(f_ref, 2 * pd + a, 2 * pr + b)
                    )
            both = grad[:64] + pltpu.roll(grad[64:], 256 - 64, 1)
            both = jnp.where((lane >= 96) & (lane < 192), both, 0.0)
            tile, off = divmod(ab * 96, 128)
            both = pltpu.roll(both, (off - 96) % 256, 1)
            tiles[tile] = tiles[tile] + both[:, :128]
            tiles[tile + 1] = tiles[tile + 1] + both[:, 128:]
        for t in range(7):
            acc[pl.ds(1792 + 64 * t, 64), :] = tiles[t]
        acc[pl.ds(2240, 64), :] = jnp.zeros((64, 128), F32)

        def remote(index, src, dst, dev):
            return pltpu.make_async_remote_copy(
                src_ref=src, dst_ref=dst, send_sem=sum_send.at[index], recv_sem=sum_recv.at[index],
                device_id=dev, device_id_type=MESH,
            )

        rows = n_plane * chunk
        other = pl.multiple_of((1 - core) * rows, 8)
        mine = pl.multiple_of(core * rows, 8)
        send1[...] = acc[pl.ds(other, rows), :].reshape(n_plane, chunk, 128).astype(LINK)
        swap = remote(0, send1, recv1, mate)
        swap.start()
        swap.wait()
        summed = acc[pl.ds(mine, rows), :].reshape(n_plane, chunk, 128) + recv1[...].astype(F32)
        half[...] = summed
        send2[...] = summed.astype(LINK)
        base = 1
        copies = []
        for s in range(1, n_plane):
            target = lax.rem(plane + s, n_plane)
            copies.append(remote(base + s, send2.at[target], recv2.at[s], plane_dev(target)))
            copies[-1].start()
        total = half[plane]
        for s in range(1, n_plane):
            copies[s - 1].wait()
            total += recv2[s].astype(F32)
        part[...] = total
        base += n_plane
        copies = []
        for k in range(n_col):
            send3[k] = part[pl.ds(k, piece, stride=n_col), :]
        for s in range(1, n_col):
            target = lax.rem(col + s, n_col)
            copies.append(remote(base + s, send3.at[target], recv3.at[s], (dep, row, target)))
            copies[-1].start()
        total = send3[col]
        for s in range(1, n_col):
            copies[s - 1].wait()
            total += recv3[s]
        tot[...] = total
        recv4[col] = total
        base += n_col
        copies = []
        for s in range(1, n_col):
            target = lax.rem(col + s, n_col)
            copies.append(remote(base + s, tot, recv4.at[col], (dep, row, target)))
            copies[-1].start()
        for copy in copies:
            copy.wait()
        for k in range(n_col):
            part[pl.ds(k, piece, stride=n_col), :] = recv4[k]
        base += n_col
        gath[core, plane] = part[...].astype(LINK)
        copies, onward = [], []
        own = gath.at[core, plane]
        for s in range(1, n_plane):
            target = lax.rem(plane + s, n_plane)
            copies.append(remote(base + s, own, own, plane_dev(target)))
            copies[-1].start()
        base += n_plane
        onward.append(remote(base, own, own, mate))
        onward[-1].start()
        for s in range(1, n_plane):
            copies[s - 1].wait()
            came = gath.at[core, lax.rem(plane - s + n_plane, n_plane)]
            onward.append(remote(base + s, came, came, mate))
            onward[-1].start()
        for copy in onward:
            copy.wait()
        for h in range(2):
            for w in range(n_plane):
                full[pl.ds((h * n_plane + w) * chunk, chunk), :] = gath[h, w].astype(F32)
        for t in range(13):
            g2_out[:, pl.ds(128 * t, 128)] = full[pl.ds(128 * t, 128), :]
        g2_out[:, pl.ds(1664, 64)] = full[pl.ds(1664, 128), pl.ds(0, 64)]
        for t in range(6):
            g1_out[:, pl.ds(128 * t, 128)] = full[pl.ds(1792 + 64 * t, 64), :]
        g1_out[:, pl.ds(768, 96)] = full[pl.ds(1792 + 384, 64), pl.ds(0, 96)]

    return kernel


def solution(mesh):
    n_dep, n_row, n_col = mesh.shape["depth"], mesh.shape["row"], mesh.shape["col"]
    n_plane = n_dep * n_row // 2
    chunk = ROWS // (2 * n_plane)
    piece = chunk // n_col
    kernel = make_kernel(n_dep, n_row, n_col)
    n_sum = 1 + 3 * n_plane + 2 * n_col + 8

    def vm(shape, dtype):
        return pltpu.VMEM(shape, dtype)

    def shards(volume, first_weight, second_weight, cotangent):
        volume = volume.reshape(8, 4, 16, 1024)
        return tuple(pl.pallas_call(
            kernel,
            out_shape=(
                jax.ShapeDtypeStruct((64, 864), F32),
                jax.ShapeDtypeStruct((128, 1728), F32),
            ),
            in_specs=[pl.BlockSpec(memory_space=pltpu.VMEM)] * 4,
            out_specs=(pl.BlockSpec(memory_space=pltpu.VMEM),) * 2,
            scratch_shapes=[
                vm((4, 9, 152, 128), F32), vm((5, 5, 9, 32, 128), BF16),
                vm((64, 896), F32), vm((128, 1792), F32),
                vm((9, 128, 256), BF16), vm((9, 128, 256), BF16), vm((8, 32, 128), F32),
                vm((8, 32, 128), BF16), vm((8, 4, 16, 128), BF16), vm((9, 32, 128), BF16),
                vm((16, 1024), BF16), vm((16, 128), BF16), vm((16, 1024), BF16), vm((16, 128), BF16),
                vm((2, 2, 9, 40, 128), F32), vm((9, 9, 32, 128), BF16), vm((2, 2, 256, 128), F32),
                vm((4, 32, 128), BF16), vm((8, 16, 128), BF16), vm((8, 16, 128), BF16),
                vm((4, 32, 128), BF16), vm((9, 16, 128), BF16), vm((9, 16, 128), BF16), vm((9, 16, 128), BF16),
                vm((9, 40, 128), F32), vm((4, 9, 32, 128), BF16), vm((128, 256), BF16), vm((128, 1024), BF16),
                vm((32, 128), BF16), vm((8, 8, 128), F32), vm((8, 8, 128), F32),
                vm((32, 128), BF16), vm((9, 8, 128), F32), vm((9, 8, 128), F32), vm((9, 8, 128), F32),
                vm((ROWS, 128), F32), vm((n_plane, chunk, 128), F32),
                vm((n_plane, chunk, 128), LINK), vm((n_plane, chunk, 128), LINK),
                vm((n_plane, chunk, 128), LINK), vm((n_plane, chunk, 128), LINK),
                vm((chunk, 128), F32), vm((n_col, piece, 128), F32), vm((n_col, piece, 128), F32),
                vm((piece, 128), F32), vm((n_col, piece, 128), F32),
                vm((2, n_plane, chunk, 128), LINK), vm((ROWS, 128), F32),
                pltpu.SemaphoreType.DMA((21,)), pltpu.SemaphoreType.DMA((21,)),
                pltpu.SemaphoreType.DMA((n_sum + n_plane,)), pltpu.SemaphoreType.DMA((n_sum + n_plane,)),
            ],
            compiler_params=pltpu.CompilerParams(
                collective_id=0, has_side_effects=True, vmem_limit_bytes=48 * 1024 * 1024
            ),
            name="sections",
        )(volume, first_weight, second_weight, cotangent))

    placed = (P("depth", "row", "col"), P(), P(), P("depth", "row", "col"))
    return jax.shard_map(shards, mesh=mesh, in_specs=placed, out_specs=(P(), P()), check_vma=False)
```

```python
import jax
import jax.numpy as jnp
from jax import lax
from jax.experimental import pallas as pl
from jax.experimental.pallas import tpu as pltpu
from jax.sharding import PartitionSpec as P

MESH = pl.DeviceIdType.MESH
F32 = jnp.float32
BF16 = jnp.bfloat16

ROWS1, ROWS2 = 512, 1792


def leaky(values):
    root = lax.rsqrt(values * values + 1.0)
    return 0.6 * values + 0.4 * ((values * values + 1.0) * root - 1.0)


def leaky_slope(values):
    return 0.6 + 0.4 * values * lax.rsqrt(values * values + 1.0)


def dot_nt(lhs, rhs):
    return lax.dot_general(lhs, rhs, (((1,), (1,)), ((), ())), preferred_element_type=F32)


def dot_tn(lhs, rhs):
    return lax.dot_general(lhs, rhs, (((0,), (0,)), ((), ())), preferred_element_type=F32)


def dot_nn(lhs, rhs):
    return lax.dot_general(lhs, rhs, (((1,), (0,)), ((), ())), preferred_element_type=F32)


def window(ref, *lead):
    low = ref[lead + (pl.ds(0, 8),)].reshape(256, 128)
    high = ref[lead + (pl.ds(1, 8),)].reshape(256, 128)
    return jnp.concatenate([low, high], axis=1)


def make_kernel(n_dep, n_row, n_col):
    n_half = n_row // 2
    n_plane = n_dep * n_half

    def kernel(
        vol_in, w1_in, w2_in, cot_in, g1_out, g2_out,
        vol, w1, w2, cot, load_sem,
        s_ref, f_ref, w1f, w1b, w2b, up,
        f_sc, f_sr, f_sk, f_c, f_r, f_d, f_dc, f_dr, f_drc,
        hs, hx, slope1, h_sc, h_sr, h_sd, h_sk, h_c, h_r, h_d, h_dc, h_dr, h_drc,
        q_ref, dx, d1t, q_sc, q_sr, q_sd, q_sk, q_c, q_r, q_rc, q_d, q_dc, q_dr, q_drc,
        acc1, swap1, send1, come1, cols1, gath1, full1,
        acc2, swap2, send2, come2, cols2, gath2,
        halo_send, halo_recv, sum_send1, sum_recv1, sum_send2, sum_recv2,
    ):
        dep, row, col = lax.axis_index("depth"), lax.axis_index("row"), lax.axis_index("col")
        core, line = lax.rem(row, 2), lax.div(row, 2)
        plane = dep * n_half + line

        loads = [
            pltpu.make_async_copy(src, dst, load_sem.at[i])
            for i, (src, dst) in enumerate(((vol_in, vol), (w1_in, w1), (w2_in, w2), (cot_in, cot)))
        ]
        for load in loads:
            load.start()

        def plane_dev(index):
            return (lax.div(index, n_half), 2 * lax.rem(index, n_half) + core, col)

        def shifted(step, d, r, c):
            return (
                lax.rem(dep + d * step + n_dep, n_dep),
                lax.rem(row + r * step + n_row, n_row),
                lax.rem(col + c * step + n_col, n_col),
            )

        mate = (dep, row + 1 - 2 * core, col)
        corners = [(d, r, c) for d in (0, 1) for r in (0, 1) for c in (0, 1)][1:]

        barrier = pltpu.get_barrier_semaphore()
        peers = [shifted(s, *e) for e in corners for s in (1, -1)]
        peers.append(mate)
        peers += [plane_dev(lax.rem(plane + s, n_plane)) for s in range(1, n_plane)]
        peers += [(dep, row, lax.rem(col + s, n_col)) for s in range(1, n_col)]
        for peer in peers:
            pl.semaphore_signal(barrier, inc=1, device_id=peer, device_id_type=MESH)

        loads[0].wait()
        for rd in range(4):
            for t in (7, 0, 1, 2, 3, 4, 5, 6):
                s_ref[rd, 1 + t, pl.ds(24, 128), :] = (
                    vol[:, rd, :, pl.ds(128 * t, 128)].astype(F32).reshape(128, 128)
                )
        for t in range(8):
            rows = [s_ref[rd, 1 + t, pl.ds(24 + 15, 8, stride=16), :] for rd in range(4)]
            f_sr[t] = jnp.concatenate(rows, axis=0).astype(BF16)
        lane = lax.broadcasted_iota(jnp.int32, (128, 128), 1)
        packed = s_ref[3, 8, pl.ds(24, 128), :]
        for rd in range(3):
            moved = pltpu.roll(s_ref[rd, 8, pl.ds(24, 128), :], 32 * rd + 32, 1)
            packed = jnp.where((lane >= 32 * rd) & (lane < 32 * rd + 32), moved, packed)
        f_sc[...] = packed.astype(BF16)
        for t in range(8):
            f_sk[pl.ds(t, 1), :] = s_ref[3, 1 + t, pl.ds(151, 1), :]

        pl.semaphore_wait(barrier, len(peers))

        def halo(phase, kind, src, dst, step):
            index = phase * 7 + kind
            return pltpu.make_async_remote_copy(
                src_ref=src, dst_ref=dst, send_sem=halo_send.at[index], recv_sem=halo_recv.at[index],
                device_id=shifted(step, *corners[kind]), device_id_type=MESH,
            )

        field_copies = [
            halo(0, 6, f_sc.at[pl.ds(112, 16)], f_drc, 1),
            halo(0, 5, f_sk, f_dr, 1),
            halo(0, 3, vol.at[7, 3], f_d, 1),
            halo(0, 4, f_sc.at[pl.ds(112, 16)], f_dc, 1),
            halo(0, 1, f_sr, f_r.at[pl.ds(1, 8)], 1),
            halo(0, 2, f_sr.at[7], f_r.at[0], 1),
            halo(0, 0, f_sc, f_c, 1),
        ]
        for copy in field_copies:
            copy.start()

        for load in loads[1:]:
            load.wait()
        w1f[:, pl.ds(768, 128)] = jnp.zeros((64, 128), F32)
        w1f[:, pl.ds(0, 864)] = w1[...].astype(F32)
        lane1 = lax.broadcasted_iota(jnp.int32, (64, 256), 1)
        for ab in range(9):
            tile, off = divmod(ab * 96, 128)
            if tile == 6:
                band = jnp.concatenate([w1f[:, pl.ds(768, 128)], jnp.zeros((64, 128), F32)], axis=1)
            else:
                band = w1f[:, pl.ds(128 * tile, 256)]
            for kk, start in ((0, 96), (1, 160)):
                moved = pltpu.roll(band, (start - off) % 256, 1)
                keep = (lane1 >= start) & (lane1 < start + 96)
                w1b[ab, pl.ds(64 * kk, 64), :] = jnp.where(keep, moved, 0.0).astype(BF16)
            w2b[ab, pl.ds(0, 64), :] = jnp.zeros((64, 128), BF16)
            w2b[ab, pl.ds(64, 192), :] = w2[pl.ds(192 * ab, 192), :]
        for i in range(8):
            line_up = cot[i].astype(F32)
            for k in range(8):
                up[k, pl.ds(4 * i, 4), :] = line_up[:, 128 * k : 128 * (k + 1)]

        def pick_field(t, rd, rr):
            source, start = (3, 8) if rd < 0 else (rd, 24)
            rows = s_ref[source, t, pl.ds(start + rr, 32, stride=4), :]
            f_ref[rd + 1, rr + 1, t] = rows.astype(BF16)

        def local_tile(t, carry):
            for rd in range(4):
                for rr in range(4):
                    pick_field(t, rd, rr)
            return carry

        lax.fori_loop(1, 9, local_tile, 0)

        for copy in field_copies:
            copy.wait_recv()

        first_dep, first_row, first_col = dep == 0, row == 0, col == 0

        def unless(edge, values):
            return jnp.where(edge, 0.0, values.astype(F32))

        packed = unless(first_col, f_c[...])
        for rd in range(4):
            s_ref[rd, 0, pl.ds(24, 128), :] = packed if rd == 3 else pltpu.roll(packed, 96 - 32 * rd, 1)
        for t in range(8):
            s_ref[3, 1 + t, pl.ds(8, 16), :] = unless(first_dep, f_d[:, pl.ds(128 * t, 128)])
        s_ref[3, 0, pl.ds(8, 16), :] = unless(first_dep | first_col, f_dc[...])
        for rd in range(4):
            for rr in range(4):
                pick_field(0, rd, rr)

        def above_tile(t, carry):
            for rr in range(4):
                pick_field(t, -1, rr)
            return carry

        lax.fori_loop(0, 9, above_tile, 0)

        def row_tile(t, carry):
            block = unless(first_row | (first_col & (t == 0)), f_r[t])
            for rd in range(4):
                s_ref[rd, t, pl.ds(23, 8, stride=16), :] = block[8 * rd : 8 * rd + 8]
            return carry

        lax.fori_loop(0, 9, row_tile, 0)
        s_ref[3, 0, pl.ds(7, 1), :] = unless(first_dep | first_row | first_col, f_drc[...])[15:16]
        block = unless(first_dep | first_row, f_dr[...])
        for t in range(8):
            s_ref[3, 1 + t, pl.ds(7, 1), :] = block[t : t + 1]

        def behind_tile(t, carry):
            for rd in range(-1, 4):
                pick_field(t, rd, -1)
            return carry

        lax.fori_loop(0, 9, behind_tile, 0)

        for pd in range(2):
            for pr in range(2):
                pre = jnp.zeros((256, 128), F32)
                for ab in range(9):
                    a, b = divmod(ab, 3)
                    pre += dot_nt(window(f_ref, 2 * pd + a, 2 * pr + b), w1b[ab])
                slope1[pd, pr] = leaky_slope(pre)
                hid = leaky(pre).reshape(8, 32, 128)
                hs[pd, pr, pl.ds(1, 8), pl.ds(8, 32), :] = hid
                h_sc[2 * pd + pr] = hid[7].astype(BF16)
        for t in range(8):
            rows = [hs[pd, 1, 1 + t, pl.ds(11, 8, stride=4), :] for pd in range(2)]
            h_sr[t] = jnp.concatenate(rows, axis=0).astype(BF16)
            h_sk[pl.ds(t, 1), :] = hs[1, 1, 1 + t, pl.ds(39, 1), :]
        for t in range(4):
            rows = [hs[1, pr, 1 + 2 * t + u, pl.ds(36, 4), :] for u in range(2) for pr in range(2)]
            h_sd[t] = jnp.concatenate(rows, axis=0).astype(BF16)
        hidden_copies = [
            halo(1, 6, h_sd.at[3], h_drc, 1),
            halo(1, 5, h_sk, h_dr, 1),
            halo(1, 3, h_sd, h_d, 1),
            halo(1, 4, h_sd.at[3], h_dc, 1),
            halo(1, 1, h_sr, h_r.at[pl.ds(1, 8)], 1),
            halo(1, 2, h_sr.at[7], h_r.at[0], 1),
            halo(1, 0, h_sc, h_c, 1),
        ]
        for copy in hidden_copies:
            copy.start()

        def pick_hidden(a, b, pd, pr, start):
            hx[3 * a + b] = hs[pd, pr, :, pl.ds(start, 32), :].astype(BF16)

        for copy in hidden_copies:
            copy.wait_recv()
        for pd in range(2):
            for pr in range(2):
                hs[pd, pr, 0, pl.ds(8, 32), :] = unless(first_col, h_c[2 * pd + pr])
        for t in range(4):
            block = unless(first_dep, h_d[t])
            for u in range(2):
                for pr in range(2):
                    start = 8 * u + 4 * pr
                    hs[1, pr, 1 + 2 * t + u, pl.ds(4, 4), :] = block[start : start + 4]
        block = unless(first_dep | first_col, h_dc[...])
        for pr in range(2):
            hs[1, pr, 0, pl.ds(4, 4), :] = block[8 + 4 * pr : 12 + 4 * pr]
        for pr in range(2):
            pick_hidden(0, 1 + pr, 1, pr, 4)
            pick_hidden(1, 1 + pr, 0, pr, 8)
            pick_hidden(2, 1 + pr, 1, pr, 8)
        for t in range(9):
            edge = first_row | first_col if t == 0 else first_row
            block = unless(edge, h_r[t])
            for pd in range(2):
                hs[pd, 1, t, pl.ds(7, 8, stride=4), :] = block[8 * pd : 8 * pd + 8]
        block = unless(first_dep | first_row, h_dr[...])
        for t in range(8):
            hs[1, 1, 1 + t, pl.ds(3, 1), :] = block[t : t + 1]
        hs[1, 1, 0, pl.ds(3, 1), :] = unless(first_dep | first_row | first_col, h_drc[...])[15:16]
        pick_hidden(0, 0, 1, 1, 3)
        pick_hidden(1, 0, 0, 1, 7)
        pick_hidden(2, 0, 1, 1, 7)

        pre = jnp.zeros((256, 128), F32)
        for ab in range(9):
            pre += dot_nn(window(hx, ab), w2b[ab])
        delta2 = up[...].reshape(256, 128) * leaky_slope(pre)
        q_ref[pl.ds(0, 8), pl.ds(0, 32), :] = delta2.reshape(8, 32, 128)
        q_sc[...] = delta2[:32].astype(BF16)
        for t in range(4):
            rows = [q_ref[2 * t + u, pl.ds(0, 8, stride=4), :] for u in range(2)]
            q_sr[t] = jnp.concatenate(rows, axis=0).astype(BF16)
            rows = [q_ref[2 * t + u, pl.ds(0, 8), :] for u in range(2)]
            q_sd[t] = jnp.concatenate(rows, axis=0).astype(BF16)
        for t in range(8):
            q_sk[pl.ds(t, 1), :] = q_ref[t, pl.ds(0, 1), :]
        delta_copies = [
            halo(2, 6, q_sd.at[0], q_drc, -1),
            halo(2, 5, q_sk, q_dr, -1),
            halo(2, 3, q_sd, q_d, -1),
            halo(2, 4, q_sd.at[0], q_dc, -1),
            halo(2, 1, q_sr, q_r, -1),
            halo(2, 2, q_sr.at[0], q_rc, -1),
            halo(2, 0, q_sc, q_c, -1),
        ]
        for copy in delta_copies:
            copy.start()

        def summing(rows, acc, swap, send, come, cols, gath, sems_out, sems_in):
            half, chunk = rows // 2, rows // (2 * n_plane)

            def remote(index, src, dst, dev):
                return pltpu.make_async_remote_copy(
                    src_ref=src, dst_ref=dst, send_sem=sems_out.at[index], recv_sem=sems_in.at[index],
                    device_id=dev, device_id_type=MESH,
                )

            order = sorted(range(1, n_plane), key=lambda s: -min(s % n_half, n_half - s % n_half))
            other = pl.multiple_of((1 - core) * half, 8)
            mine = pl.multiple_of(core * half, 8)
            first = remote(0, acc.at[pl.ds(other, half)], swap, mate)
            spread, around, back, onward = {}, {}, {}, {}
            own = gath.at[core, plane]
            for s in order:
                target = lax.rem(plane + s, n_plane)
                spread[s] = remote(s, send.at[target], come.at[s], plane_dev(target))
                back[s] = remote(n_plane + s, own, own, plane_dev(target))
                came = gath.at[core, lax.rem(plane - s + n_plane, n_plane)]
                onward[s] = remote(2 * n_plane + s, came, came, mate)
            onward[0] = remote(2 * n_plane, own, own, mate)
            for s in range(1, n_col):
                target = lax.rem(col + s, n_col)
                around[s] = remote(3 * n_plane + s, cols.at[col], cols.at[col], (dep, row, target))

            def to_plane():
                first.wait_recv()
                summed = acc[pl.ds(mine, half), :] + swap[...]
                send[...] = summed.reshape(n_plane, chunk, 128).astype(BF16)
                for s in order:
                    spread[s].start()

            def to_column():
                place = pl.multiple_of(plane * chunk, 8)
                total = acc[pl.ds(mine + place, chunk), :] + swap[pl.ds(place, chunk), :]
                for s in reversed(order):
                    spread[s].wait_recv()
                    total += come[s].astype(F32)
                cols[col] = total.astype(BF16)
                for s in sorted(around, key=lambda s: -min(s, n_col - s)):
                    around[s].start()

            def to_all():
                for s in around:
                    around[s].wait_recv()
                total = cols[0].astype(F32)
                for k in range(1, n_col):
                    total += cols[k].astype(F32)
                gath[core, plane] = total.astype(BF16)
                for s in order:
                    back[s].start()
                onward[0].start()

            def to_mate():
                for s in reversed(order):
                    back[s].wait_recv()
                    onward[s].start()

            def finish():
                for s in onward:
                    onward[s].wait_recv()

            def drain():
                first.wait_send()
                for group in (spread, around, back, onward):
                    for s in group:
                        group[s].wait_send()

            return first.start, to_plane, to_column, to_all, to_mate, finish, drain

        sum1 = summing(ROWS1, acc1, swap1, send1, come1, cols1, gath1, sum_send1, sum_recv1)
        sum2 = summing(ROWS2, acc2, swap2, send2, come2, cols2, gath2, sum_send2, sum_recv2)

        flat2 = delta2.astype(BF16)
        for ab in range(9):
            acc2[pl.ds(192 * ab, 192), :] = dot_tn(window(hx, ab), flat2)[64:]
        acc2[pl.ds(1728, 64), :] = jnp.zeros((64, 128), F32)
        sum2[0]()
        sum2[1]()

        for copy in delta_copies:
            copy.wait_recv()
        last_dep, last_row, last_col = dep == n_dep - 1, row == n_row - 1, col == n_col - 1
        q_ref[8, pl.ds(0, 32), :] = unless(last_col, q_c[...])
        for t in range(8):
            u = 8 * (t % 2)
            q_ref[t, pl.ds(32, 4), :] = unless(last_dep, q_d[t // 2])[u : u + 4]
        q_ref[8, pl.ds(32, 4), :] = unless(last_dep | last_col, q_dc[...])[:4]
        dx[0] = q_ref[:, pl.ds(0, 32), :].astype(BF16)
        dx[2] = q_ref[:, pl.ds(4, 32), :].astype(BF16)
        for t in range(8):
            u = 8 * (t % 2)
            q_ref[t, pl.ds(4, 8, stride=4), :] = unless(last_row, q_r[t // 2])[u : u + 8]
        q_ref[8, pl.ds(4, 8, stride=4), :] = unless(last_row | last_col, q_rc[...])[:8]
        block = unless(last_dep | last_row, q_dr[...])
        for t in range(8):
            q_ref[t, pl.ds(36, 1), :] = block[t : t + 1]
        q_ref[8, pl.ds(36, 1), :] = unless(last_dep | last_row | last_col, q_drc[...])[:1]
        dx[1] = q_ref[:, pl.ds(1, 32), :].astype(BF16)
        dx[3] = q_ref[:, pl.ds(5, 32), :].astype(BF16)

        taps = (((1, 0),), ((2, 0), (0, 1)))
        for pd in range(2):
            for pr in range(2):
                back = jnp.zeros((256, 128), F32)
                for a, od in taps[pd]:
                    for b, o_r in taps[pr]:
                        band = jnp.concatenate(
                            [w2b[3 * a + b, pl.ds(128, 128), :], w2b[3 * a + b, pl.ds(0, 128), :]], axis=1
                        )
                        back += dot_nt(window(dx, 2 * od + o_r), band)
                delta1 = back * slope1[pd, pr]
                d1t[:, pl.ds(512 * pd + 256 * pr, 256)] = delta1.T.astype(BF16)

        lane = lax.broadcasted_iota(jnp.int32, (64, 256), 1)
        tiles = [jnp.zeros((64, 128), F32) for _ in range(8)]
        for ab in range(9):
            a, b = divmod(ab, 3)
            grad = jnp.zeros((128, 256), F32)
            for pd in range(2):
                for pr in range(2):
                    grad += dot_nn(
                        d1t[:, pl.ds(512 * pd + 256 * pr, 256)], window(f_ref, 2 * pd + a, 2 * pr + b)
                    )
            both = grad[:64] + pltpu.roll(grad[64:], 256 - 64, 1)
            both = jnp.where((lane >= 96) & (lane < 192), both, 0.0)
            tile, off = divmod(ab * 96, 128)
            both = pltpu.roll(both, (off - 96) % 256, 1)
            tiles[tile] = tiles[tile] + both[:, :128]
            tiles[tile + 1] = tiles[tile + 1] + both[:, 128:]
        for t in range(8):
            acc1[pl.ds(64 * t, 64), :] = tiles[t]

        sum1[0]()
        sum2[2]()
        sum1[1]()
        sum2[3]()
        sum1[2]()
        sum2[4]()
        sum1[3]()
        sum2[5]()
        chunk1, chunk2 = ROWS1 // (2 * n_plane), ROWS2 // (2 * n_plane)
        for h in range(2):
            for w in range(n_plane):
                start = (h * n_plane + w) * chunk2
                size = min(chunk2, 1728 - start)
                if size > 0:
                    g2_out[pl.ds(start, size), :] = gath2[h, w].astype(F32)[:size]
        sum1[4]()
        sum1[5]()
        for h in range(2):
            for w in range(n_plane):
                full1[pl.ds((h * n_plane + w) * chunk1, chunk1), :] = gath1[h, w].astype(F32)
        for t in range(6):
            g1_out[:, pl.ds(128 * t, 128)] = full1[pl.ds(64 * t, 64), :]
        g1_out[:, pl.ds(768, 96)] = full1[pl.ds(384, 64), pl.ds(0, 96)]
        sum1[6]()
        sum2[6]()
        for copy in field_copies + hidden_copies + delta_copies:
            copy.wait_send()

    return kernel


def solution(mesh):
    n_dep, n_row, n_col = mesh.shape["depth"], mesh.shape["row"], mesh.shape["col"]
    n_plane = n_dep * n_row // 2
    kernel = make_kernel(n_dep, n_row, n_col)
    n_sum = 3 * n_plane + n_col

    def vm(shape, dtype):
        return pltpu.VMEM(shape, dtype)

    def sum_scratch(rows):
        half, chunk = rows // 2, rows // (2 * n_plane)
        return [
            vm((rows, 128), F32), vm((half, 128), F32),
            vm((n_plane, chunk, 128), BF16), vm((n_plane, chunk, 128), BF16),
            vm((n_col, chunk, 128), BF16), vm((2, n_plane, chunk, 128), BF16),
        ]

    def shards(volume, first_weight, second_weight, cotangent):
        first_grad, second_grad = pl.pallas_call(
            kernel,
            out_shape=(
                jax.ShapeDtypeStruct((64, 864), F32),
                jax.ShapeDtypeStruct((1728, 128), F32),
            ),
            in_specs=[pl.BlockSpec(memory_space=pltpu.HBM)] * 4,
            out_specs=(pl.BlockSpec(memory_space=pltpu.VMEM),) * 2,
            scratch_shapes=[
                vm((8, 4, 16, 1024), BF16), vm((64, 864), BF16), vm((1728, 128), BF16), vm((8, 4, 1024), BF16),
                pltpu.SemaphoreType.DMA((4,)),
                vm((4, 9, 152, 128), F32), vm((5, 5, 9, 32, 128), BF16),
                vm((64, 896), F32), vm((9, 128, 256), BF16), vm((9, 256, 128), BF16), vm((8, 32, 128), F32),
                vm((128, 128), BF16), vm((8, 32, 128), BF16), vm((8, 128), F32),
                vm((128, 128), BF16), vm((9, 32, 128), BF16), vm((16, 1024), BF16), vm((16, 128), BF16),
                vm((8, 128), F32), vm((16, 128), BF16),
                vm((2, 2, 9, 40, 128), F32), vm((9, 9, 32, 128), BF16), vm((2, 2, 256, 128), F32),
                vm((4, 32, 128), BF16), vm((8, 16, 128), BF16), vm((4, 16, 128), BF16), vm((8, 128), F32),
                vm((4, 32, 128), BF16), vm((9, 16, 128), BF16), vm((4, 16, 128), BF16), vm((16, 128), BF16),
                vm((8, 128), F32), vm((16, 128), BF16),
                vm((9, 40, 128), F32), vm((4, 9, 32, 128), BF16), vm((128, 1024), BF16),
                vm((32, 128), BF16), vm((4, 16, 128), BF16), vm((4, 16, 128), BF16), vm((8, 128), F32),
                vm((32, 128), BF16), vm((4, 16, 128), BF16), vm((16, 128), BF16),
                vm((4, 16, 128), BF16), vm((16, 128), BF16), vm((8, 128), F32), vm((16, 128), BF16),
                *sum_scratch(ROWS1), vm((ROWS1, 128), F32), *sum_scratch(ROWS2),
                pltpu.SemaphoreType.DMA((21,)), pltpu.SemaphoreType.DMA((21,)),
                pltpu.SemaphoreType.DMA((n_sum,)), pltpu.SemaphoreType.DMA((n_sum,)),
                pltpu.SemaphoreType.DMA((n_sum,)), pltpu.SemaphoreType.DMA((n_sum,)),
            ],
            compiler_params=pltpu.CompilerParams(
                collective_id=0, has_side_effects=True, vmem_limit_bytes=48 * 1024 * 1024
            ),
            name="sections",
        )(*[
            pltpu.with_memory_space_constraint(x, pltpu.HBM)
            for x in (volume.reshape(8, 4, 16, 1024), first_weight, second_weight.T, cotangent)
        ])
        return first_grad, second_grad.T

    placed = (P("depth", "row", "col"), P(), P(), P("depth", "row", "col"))
    return jax.shard_map(shards, mesh=mesh, in_specs=placed, out_specs=(P(), P()), check_vma=False)
```

```python
import jax
import jax.numpy as jnp
from jax import lax
from jax.experimental import pallas as pl
from jax.experimental.pallas import tpu as pltpu
from jax.sharding import PartitionSpec as P

MESH = pl.DeviceIdType.MESH
F32 = jnp.float32
BF16 = jnp.bfloat16

ROWS1, ROWS2 = 512, 1792


def leaky(values):
    root = lax.rsqrt(values * values + 1.0)
    return 0.6 * values + 0.4 * ((values * values + 1.0) * root - 1.0)


def leaky_slope(values):
    return 0.6 + 0.4 * values * lax.rsqrt(values * values + 1.0)


def dot_nt(lhs, rhs):
    return lax.dot_general(lhs, rhs, (((1,), (1,)), ((), ())), preferred_element_type=F32)


def dot_tn(lhs, rhs):
    return lax.dot_general(lhs, rhs, (((0,), (0,)), ((), ())), preferred_element_type=F32)


def dot_nn(lhs, rhs):
    return lax.dot_general(lhs, rhs, (((1,), (0,)), ((), ())), preferred_element_type=F32)


def window(ref, *lead):
    low = ref[lead + (pl.ds(0, 8),)].reshape(256, 128)
    high = ref[lead + (pl.ds(1, 8),)].reshape(256, 128)
    return jnp.concatenate([low, high], axis=1)


def make_kernel(n_dep, n_row, n_col):
    n_half = n_row // 2
    n_plane = n_dep * n_half

    def kernel(
        vol_in, w1_in, w2_in, cot_in, g1_out, g2_out,
        vol, w1, w2, cot, load_sem,
        s_ref, f_ref, w1f, w1b, w2b, up,
        f_sc, f_sr, f_sk, f_c, f_r, f_d, f_dc, f_dr, f_drc,
        hs, hx, slope1, h_sc, h_sr, h_sd, h_sk, h_c, h_r, h_d, h_dc, h_dr, h_drc,
        q_ref, dx, d1t, q_sc, q_sr, q_sd, q_sk, q_c, q_r, q_rc, q_d, q_dc, q_dr, q_drc,
        acc1, swap1, send1, come1, cols1, gath1, full1,
        acc2, swap2, send2, come2, cols2, gath2,
        halo_send, halo_recv, sum_send1, sum_recv1, sum_send2, sum_recv2,
    ):
        dep, row, col = lax.axis_index("depth"), lax.axis_index("row"), lax.axis_index("col")
        core, line = lax.rem(row, 2), lax.div(row, 2)
        plane = dep * n_half + line

        loads = [
            pltpu.make_async_copy(src, dst, load_sem.at[i])
            for i, (src, dst) in enumerate(((vol_in, vol), (w1_in, w1), (w2_in, w2), (cot_in, cot)))
        ]
        for load in loads:
            load.start()

        def plane_dev(index):
            return (lax.div(index, n_half), 2 * lax.rem(index, n_half) + core, col)

        def shifted(step, d, r, c):
            return (
                lax.rem(dep + d * step + n_dep, n_dep),
                lax.rem(row + r * step + n_row, n_row),
                lax.rem(col + c * step + n_col, n_col),
            )

        mate = (dep, row + 1 - 2 * core, col)
        corners = [(d, r, c) for d in (0, 1) for r in (0, 1) for c in (0, 1)][1:]

        barrier = pltpu.get_barrier_semaphore()
        peers = [shifted(s, *e) for e in corners for s in (1, -1)]
        peers.append(mate)
        peers += [plane_dev(lax.rem(plane + s, n_plane)) for s in range(1, n_plane)]
        peers += [(dep, row, lax.rem(col + s, n_col)) for s in range(1, n_col)]
        for peer in peers:
            pl.semaphore_signal(barrier, inc=1, device_id=peer, device_id_type=MESH)

        loads[0].wait()
        for rd in range(4):
            for t in (7, 0, 1, 2, 3, 4, 5, 6):
                s_ref[rd, 1 + t, pl.ds(24, 128), :] = (
                    vol[:, rd, :, pl.ds(128 * t, 128)].astype(F32).reshape(128, 128)
                )
        for t in range(8):
            rows = [s_ref[rd, 1 + t, pl.ds(24 + 15, 8, stride=16), :] for rd in range(4)]
            f_sr[t] = jnp.concatenate(rows, axis=0).astype(BF16)
        lane = lax.broadcasted_iota(jnp.int32, (128, 128), 1)
        packed = s_ref[3, 8, pl.ds(24, 128), :]
        for rd in range(3):
            moved = pltpu.roll(s_ref[rd, 8, pl.ds(24, 128), :], 32 * rd + 32, 1)
            packed = jnp.where((lane >= 32 * rd) & (lane < 32 * rd + 32), moved, packed)
        f_sc[...] = packed.astype(BF16)
        for t in range(8):
            f_sk[pl.ds(t, 1), :] = s_ref[3, 1 + t, pl.ds(151, 1), :]

        pl.semaphore_wait(barrier, len(peers))

        def halo(phase, kind, src, dst, step):
            index = phase * 7 + kind
            return pltpu.make_async_remote_copy(
                src_ref=src, dst_ref=dst, send_sem=halo_send.at[index], recv_sem=halo_recv.at[index],
                device_id=shifted(step, *corners[kind]), device_id_type=MESH,
            )

        field_copies = [
            halo(0, 6, f_sc.at[pl.ds(112, 16)], f_drc, 1),
            halo(0, 5, f_sk, f_dr, 1),
            halo(0, 3, vol.at[7, 3], f_d, 1),
            halo(0, 4, f_sc.at[pl.ds(112, 16)], f_dc, 1),
            halo(0, 1, f_sr, f_r.at[pl.ds(1, 8)], 1),
            halo(0, 2, f_sr.at[7], f_r.at[0], 1),
            halo(0, 0, f_sc, f_c, 1),
        ]
        for copy in field_copies:
            copy.start()

        for load in loads[1:]:
            load.wait()
        w1f[:, pl.ds(768, 128)] = jnp.zeros((64, 128), F32)
        w1f[:, pl.ds(0, 864)] = w1[...].astype(F32)
        lane1 = lax.broadcasted_iota(jnp.int32, (64, 256), 1)
        for ab in range(9):
            tile, off = divmod(ab * 96, 128)
            if tile == 6:
                band = jnp.concatenate([w1f[:, pl.ds(768, 128)], jnp.zeros((64, 128), F32)], axis=1)
            else:
                band = w1f[:, pl.ds(128 * tile, 256)]
            for kk, start in ((0, 96), (1, 160)):
                moved = pltpu.roll(band, (start - off) % 256, 1)
                keep = (lane1 >= start) & (lane1 < start + 96)
                w1b[ab, pl.ds(64 * kk, 64), :] = jnp.where(keep, moved, 0.0).astype(BF16)
            w2b[ab, pl.ds(0, 64), :] = jnp.zeros((64, 128), BF16)
            w2b[ab, pl.ds(64, 192), :] = w2[pl.ds(192 * ab, 192), :]
        for i in range(8):
            line_up = cot[i].astype(F32)
            for k in range(8):
                up[k, pl.ds(4 * i, 4), :] = line_up[:, 128 * k : 128 * (k + 1)]

        def pick_field(t, rd, rr):
            source, start = (3, 8) if rd < 0 else (rd, 24)
            rows = s_ref[source, t, pl.ds(start + rr, 32, stride=4), :]
            f_ref[rd + 1, rr + 1, t] = rows.astype(BF16)

        def local_tile(t, carry):
            for rd in range(4):
                for rr in range(4):
                    pick_field(t, rd, rr)
            return carry

        lax.fori_loop(1, 9, local_tile, 0)

        for copy in field_copies:
            copy.wait_recv()

        first_dep, first_row, first_col = dep == 0, row == 0, col == 0

        def unless(edge, values):
            return jnp.where(edge, 0.0, values.astype(F32))

        packed = unless(first_col, f_c[...])
        for rd in range(4):
            s_ref[rd, 0, pl.ds(24, 128), :] = packed if rd == 3 else pltpu.roll(packed, 96 - 32 * rd, 1)
        for t in range(8):
            s_ref[3, 1 + t, pl.ds(8, 16), :] = unless(first_dep, f_d[:, pl.ds(128 * t, 128)])
        s_ref[3, 0, pl.ds(8, 16), :] = unless(first_dep | first_col, f_dc[...])
        for rd in range(4):
            for rr in range(4):
                pick_field(0, rd, rr)

        def above_tile(t, carry):
            for rr in range(4):
                pick_field(t, -1, rr)
            return carry

        lax.fori_loop(0, 9, above_tile, 0)

        def row_tile(t, carry):
            block = unless(first_row | (first_col & (t == 0)), f_r[t])
            for rd in range(4):
                s_ref[rd, t, pl.ds(23, 8, stride=16), :] = block[8 * rd : 8 * rd + 8]
            return carry

        lax.fori_loop(0, 9, row_tile, 0)
        s_ref[3, 0, pl.ds(7, 1), :] = unless(first_dep | first_row | first_col, f_drc[...])[15:16]
        block = unless(first_dep | first_row, f_dr[...])
        for t in range(8):
            s_ref[3, 1 + t, pl.ds(7, 1), :] = block[t : t + 1]

        def behind_tile(t, carry):
            for rd in range(-1, 4):
                pick_field(t, rd, -1)
            return carry

        lax.fori_loop(0, 9, behind_tile, 0)

        def first_section(pd, pr):
            pre = jnp.zeros((256, 128), F32)
            for ab in range(9):
                a, b = divmod(ab, 3)
                pre += dot_nt(window(f_ref, 2 * pd + a, 2 * pr + b), w1b[ab])
            hid = leaky(pre).reshape(8, 32, 128)
            hs[pd, pr, pl.ds(1, 8), pl.ds(8, 32), :] = hid
            slope1[pd, pr] = leaky_slope(pre)
            h_sc[2 * pd + pr] = hid[7].astype(BF16)

        hidden_copies = [
            halo(1, 6, h_sk, h_drc, 1),
            halo(1, 5, h_sk, h_dr, 1),
            halo(1, 1, h_sr, h_r.at[pl.ds(1, 8)], 1),
            halo(1, 2, h_sr.at[7], h_r.at[0], 1),
            halo(1, 3, h_sd, h_d, 1),
            halo(1, 4, h_sd.at[3], h_dc, 1),
            halo(1, 0, h_sc, h_c, 1),
        ]
        first_section(1, 1)
        for t in range(8):
            h_sk[pl.ds(t, 1), :] = hs[1, 1, 1 + t, pl.ds(39, 1), :]
        for copy in hidden_copies[:2]:
            copy.start()
        first_section(0, 1)
        for t in range(8):
            rows = [hs[pd, 1, 1 + t, pl.ds(11, 8, stride=4), :] for pd in range(2)]
            h_sr[t] = jnp.concatenate(rows, axis=0).astype(BF16)
        for copy in hidden_copies[2:4]:
            copy.start()
        first_section(1, 0)
        for t in range(4):
            rows = [hs[1, pr, 1 + 2 * t + u, pl.ds(36, 4), :] for u in range(2) for pr in range(2)]
            h_sd[t] = jnp.concatenate(rows, axis=0).astype(BF16)
        for copy in hidden_copies[4:6]:
            copy.start()
        first_section(0, 0)
        hidden_copies[6].start()

        def pick_hidden(a, b, pd, pr, start):
            hx[3 * a + b] = hs[pd, pr, :, pl.ds(start, 32), :].astype(BF16)

        for copy in hidden_copies:
            copy.wait_recv()
        for pd in range(2):
            for pr in range(2):
                hs[pd, pr, 0, pl.ds(8, 32), :] = unless(first_col, h_c[2 * pd + pr])
        for t in range(4):
            block = unless(first_dep, h_d[t])
            for u in range(2):
                for pr in range(2):
                    start = 8 * u + 4 * pr
                    hs[1, pr, 1 + 2 * t + u, pl.ds(4, 4), :] = block[start : start + 4]
        block = unless(first_dep | first_col, h_dc[...])
        for pr in range(2):
            hs[1, pr, 0, pl.ds(4, 4), :] = block[8 + 4 * pr : 12 + 4 * pr]
        for pr in range(2):
            pick_hidden(0, 1 + pr, 1, pr, 4)
            pick_hidden(1, 1 + pr, 0, pr, 8)
            pick_hidden(2, 1 + pr, 1, pr, 8)
        for t in range(9):
            edge = first_row | first_col if t == 0 else first_row
            block = unless(edge, h_r[t])
            for pd in range(2):
                hs[pd, 1, t, pl.ds(7, 8, stride=4), :] = block[8 * pd : 8 * pd + 8]
        block = unless(first_dep | first_row, h_dr[...])
        for t in range(8):
            hs[1, 1, 1 + t, pl.ds(3, 1), :] = block[t : t + 1]
        hs[1, 1, 0, pl.ds(3, 1), :] = unless(first_dep | first_row | first_col, h_drc[...])[7:8]
        pick_hidden(0, 0, 1, 1, 3)
        pick_hidden(1, 0, 0, 1, 7)
        pick_hidden(2, 0, 1, 1, 7)

        pre = jnp.zeros((256, 128), F32)
        for ab in range(9):
            pre += dot_nn(window(hx, ab), w2b[ab])
        delta2 = up[...].reshape(256, 128) * leaky_slope(pre)
        q_ref[pl.ds(0, 8), pl.ds(0, 32), :] = delta2.reshape(8, 32, 128)
        q_sc[...] = delta2[:32].astype(BF16)
        for t in range(4):
            rows = [q_ref[2 * t + u, pl.ds(0, 8, stride=4), :] for u in range(2)]
            q_sr[t] = jnp.concatenate(rows, axis=0).astype(BF16)
            rows = [q_ref[2 * t + u, pl.ds(0, 8), :] for u in range(2)]
            q_sd[t] = jnp.concatenate(rows, axis=0).astype(BF16)
        for t in range(8):
            q_sk[pl.ds(t, 1), :] = q_ref[t, pl.ds(0, 1), :]
        delta_copies = [
            halo(2, 6, q_sd.at[0], q_drc, -1),
            halo(2, 5, q_sk, q_dr, -1),
            halo(2, 3, q_sd, q_d, -1),
            halo(2, 4, q_sd.at[0], q_dc, -1),
            halo(2, 1, q_sr, q_r, -1),
            halo(2, 2, q_sr.at[0], q_rc, -1),
            halo(2, 0, q_sc, q_c, -1),
        ]
        for copy in delta_copies:
            copy.start()

        def summing(rows, acc, swap, send, come, cols, gath, sems_out, sems_in):
            half, chunk = rows // 2, rows // (2 * n_plane)

            def remote(index, src, dst, dev):
                return pltpu.make_async_remote_copy(
                    src_ref=src, dst_ref=dst, send_sem=sems_out.at[index], recv_sem=sems_in.at[index],
                    device_id=dev, device_id_type=MESH,
                )

            order = sorted(range(1, n_plane), key=lambda s: -min(s % n_half, n_half - s % n_half))
            other = pl.multiple_of((1 - core) * half, 8)
            mine = pl.multiple_of(core * half, 8)
            first = remote(0, acc.at[pl.ds(other, half)], swap, mate)
            spread, around, back, onward = {}, {}, {}, {}
            own = gath.at[core, plane]
            for s in order:
                target = lax.rem(plane + s, n_plane)
                spread[s] = remote(s, send.at[target], come.at[s], plane_dev(target))
                back[s] = remote(n_plane + s, own, own, plane_dev(target))
                came = gath.at[core, lax.rem(plane - s + n_plane, n_plane)]
                onward[s] = remote(2 * n_plane + s, came, came, mate)
            onward[0] = remote(2 * n_plane, own, own, mate)
            for s in range(1, n_col):
                target = lax.rem(col + s, n_col)
                around[s] = remote(3 * n_plane + s, cols.at[col], cols.at[col], (dep, row, target))

            def to_plane():
                first.wait_recv()
                summed = acc[pl.ds(mine, half), :] + swap[...]
                send[...] = summed.reshape(n_plane, chunk, 128).astype(BF16)
                for s in order:
                    spread[s].start()

            def to_column():
                place = pl.multiple_of(plane * chunk, 8)
                total = acc[pl.ds(mine + place, chunk), :] + swap[pl.ds(place, chunk), :]
                for s in reversed(order):
                    spread[s].wait_recv()
                    total += come[s].astype(F32)
                cols[col] = total.astype(BF16)
                for s in sorted(around, key=lambda s: -min(s, n_col - s)):
                    around[s].start()

            def to_all():
                for s in around:
                    around[s].wait_recv()
                total = cols[0].astype(F32)
                for k in range(1, n_col):
                    total += cols[k].astype(F32)
                gath[core, plane] = total.astype(BF16)
                for s in order:
                    back[s].start()
                onward[0].start()

            def to_mate():
                for s in reversed(order):
                    back[s].wait_recv()
                    onward[s].start()

            def finish():
                for s in onward:
                    onward[s].wait_recv()

            def drain():
                first.wait_send()
                for group in (spread, around, back, onward):
                    for s in group:
                        group[s].wait_send()

            return first.start, to_plane, to_column, to_all, to_mate, finish, drain

        sum1 = summing(ROWS1, acc1, swap1, send1, come1, cols1, gath1, sum_send1, sum_recv1)
        sum2 = summing(ROWS2, acc2, swap2, send2, come2, cols2, gath2, sum_send2, sum_recv2)

        flat2 = delta2.astype(BF16)
        for ab in range(9):
            acc2[pl.ds(192 * ab, 192), :] = dot_tn(window(hx, ab), flat2)[64:]
        acc2[pl.ds(1728, 64), :] = jnp.zeros((64, 128), F32)
        sum2[0]()
        sum2[1]()

        for copy in delta_copies:
            copy.wait_recv()
        last_dep, last_row, last_col = dep == n_dep - 1, row == n_row - 1, col == n_col - 1
        q_ref[8, pl.ds(0, 32), :] = unless(last_col, q_c[...])
        for t in range(8):
            u = 8 * (t % 2)
            q_ref[t, pl.ds(32, 4), :] = unless(last_dep, q_d[t // 2])[u : u + 4]
        q_ref[8, pl.ds(32, 4), :] = unless(last_dep | last_col, q_dc[...])[:4]
        dx[0] = q_ref[:, pl.ds(0, 32), :].astype(BF16)
        dx[2] = q_ref[:, pl.ds(4, 32), :].astype(BF16)
        for t in range(8):
            u = 8 * (t % 2)
            q_ref[t, pl.ds(4, 8, stride=4), :] = unless(last_row, q_r[t // 2])[u : u + 8]
        q_ref[8, pl.ds(4, 8, stride=4), :] = unless(last_row | last_col, q_rc[...])[:8]
        block = unless(last_dep | last_row, q_dr[...])
        for t in range(8):
            q_ref[t, pl.ds(36, 1), :] = block[t : t + 1]
        q_ref[8, pl.ds(36, 1), :] = unless(last_dep | last_row | last_col, q_drc[...])[:1]
        dx[1] = q_ref[:, pl.ds(1, 32), :].astype(BF16)
        dx[3] = q_ref[:, pl.ds(5, 32), :].astype(BF16)

        taps = (((1, 0),), ((2, 0), (0, 1)))
        for pd in range(2):
            for pr in range(2):
                back = jnp.zeros((256, 128), F32)
                for a, od in taps[pd]:
                    for b, o_r in taps[pr]:
                        band = jnp.concatenate(
                            [w2b[3 * a + b, pl.ds(128, 128), :], w2b[3 * a + b, pl.ds(0, 128), :]], axis=1
                        )
                        back += dot_nt(window(dx, 2 * od + o_r), band)
                delta1 = back * slope1[pd, pr]
                d1t[:, pl.ds(512 * pd + 256 * pr, 256)] = delta1.T.astype(BF16)

        lane = lax.broadcasted_iota(jnp.int32, (64, 256), 1)
        tiles = [jnp.zeros((64, 128), F32) for _ in range(8)]
        for ab in range(9):
            a, b = divmod(ab, 3)
            grad = jnp.zeros((128, 256), F32)
            for pd in range(2):
                for pr in range(2):
                    grad += dot_nn(
                        d1t[:, pl.ds(512 * pd + 256 * pr, 256)], window(f_ref, 2 * pd + a, 2 * pr + b)
                    )
            both = grad[:64] + pltpu.roll(grad[64:], 256 - 64, 1)
            both = jnp.where((lane >= 96) & (lane < 192), both, 0.0)
            tile, off = divmod(ab * 96, 128)
            both = pltpu.roll(both, (off - 96) % 256, 1)
            tiles[tile] = tiles[tile] + both[:, :128]
            tiles[tile + 1] = tiles[tile + 1] + both[:, 128:]
        for t in range(8):
            acc1[pl.ds(64 * t, 64), :] = tiles[t]

        sum1[0]()
        sum1[1]()
        sum2[2]()
        sum1[2]()
        sum2[3]()
        sum1[3]()
        sum2[4]()
        sum1[4]()
        sum2[5]()
        chunk1, chunk2 = ROWS1 // (2 * n_plane), ROWS2 // (2 * n_plane)
        for h in range(2):
            for w in range(n_plane):
                start = (h * n_plane + w) * chunk2
                size = min(chunk2, 1728 - start)
                if size > 0:
                    g2_out[pl.ds(start, size), :] = gath2[h, w].astype(F32)[:size]
        sum1[5]()
        for h in range(2):
            for w in range(n_plane):
                full1[pl.ds((h * n_plane + w) * chunk1, chunk1), :] = gath1[h, w].astype(F32)
        for t in range(6):
            g1_out[:, pl.ds(128 * t, 128)] = full1[pl.ds(64 * t, 64), :]
        g1_out[:, pl.ds(768, 96)] = full1[pl.ds(384, 64), pl.ds(0, 96)]
        sum1[6]()
        sum2[6]()
        for copy in field_copies + hidden_copies + delta_copies:
            copy.wait_send()

    return kernel


def solution(mesh):
    n_dep, n_row, n_col = mesh.shape["depth"], mesh.shape["row"], mesh.shape["col"]
    n_plane = n_dep * n_row // 2
    kernel = make_kernel(n_dep, n_row, n_col)
    n_sum = 3 * n_plane + n_col

    def vm(shape, dtype):
        return pltpu.VMEM(shape, dtype)

    def sum_scratch(rows):
        half, chunk = rows // 2, rows // (2 * n_plane)
        return [
            vm((rows, 128), F32), vm((half, 128), F32),
            vm((n_plane, chunk, 128), BF16), vm((n_plane, chunk, 128), BF16),
            vm((n_col, chunk, 128), BF16), vm((2, n_plane, chunk, 128), BF16),
        ]

    def shards(volume, first_weight, second_weight, cotangent):
        first_grad, second_grad = pl.pallas_call(
            kernel,
            out_shape=(
                jax.ShapeDtypeStruct((64, 864), F32),
                jax.ShapeDtypeStruct((1728, 128), F32),
            ),
            in_specs=[pl.BlockSpec(memory_space=pltpu.HBM)] * 4,
            out_specs=(pl.BlockSpec(memory_space=pltpu.VMEM),) * 2,
            scratch_shapes=[
                vm((8, 4, 16, 1024), BF16), vm((64, 864), BF16), vm((1728, 128), BF16), vm((8, 4, 1024), BF16),
                pltpu.SemaphoreType.DMA((4,)),
                vm((4, 9, 152, 128), F32), vm((5, 5, 9, 32, 128), BF16),
                vm((64, 896), F32), vm((9, 128, 256), BF16), vm((9, 256, 128), BF16), vm((8, 32, 128), F32),
                vm((128, 128), BF16), vm((8, 32, 128), BF16), vm((8, 128), F32),
                vm((128, 128), BF16), vm((9, 32, 128), BF16), vm((16, 1024), BF16), vm((16, 128), BF16),
                vm((8, 128), F32), vm((16, 128), BF16),
                vm((2, 2, 9, 40, 128), F32), vm((9, 9, 32, 128), BF16), vm((2, 2, 256, 128), F32),
                vm((4, 32, 128), BF16), vm((8, 16, 128), BF16), vm((4, 16, 128), BF16), vm((8, 128), F32),
                vm((4, 32, 128), BF16), vm((9, 16, 128), BF16), vm((4, 16, 128), BF16), vm((16, 128), BF16),
                vm((8, 128), F32), vm((8, 128), F32),
                vm((9, 40, 128), F32), vm((4, 9, 32, 128), BF16), vm((128, 1024), BF16),
                vm((32, 128), BF16), vm((4, 16, 128), BF16), vm((4, 16, 128), BF16), vm((8, 128), F32),
                vm((32, 128), BF16), vm((4, 16, 128), BF16), vm((16, 128), BF16),
                vm((4, 16, 128), BF16), vm((16, 128), BF16), vm((8, 128), F32), vm((16, 128), BF16),
                *sum_scratch(ROWS1), vm((ROWS1, 128), F32), *sum_scratch(ROWS2),
                pltpu.SemaphoreType.DMA((21,)), pltpu.SemaphoreType.DMA((21,)),
                pltpu.SemaphoreType.DMA((n_sum,)), pltpu.SemaphoreType.DMA((n_sum,)),
                pltpu.SemaphoreType.DMA((n_sum,)), pltpu.SemaphoreType.DMA((n_sum,)),
            ],
            compiler_params=pltpu.CompilerParams(
                collective_id=0, has_side_effects=True, vmem_limit_bytes=48 * 1024 * 1024
            ),
            name="sections",
        )(*[
            pltpu.with_memory_space_constraint(x, pltpu.HBM)
            for x in (volume.reshape(8, 4, 16, 1024), first_weight, second_weight.T, cotangent)
        ])
        return first_grad, second_grad.T

    placed = (P("depth", "row", "col"), P(), P(), P("depth", "row", "col"))
    return jax.shard_map(shards, mesh=mesh, in_specs=placed, out_specs=(P(), P()), check_vma=False)
```

```python
import jax
import jax.numpy as jnp
from jax import lax
from jax.experimental import pallas as pl
from jax.experimental.pallas import tpu as pltpu
from jax.sharding import PartitionSpec as P

MESH = pl.DeviceIdType.MESH
F32 = jnp.float32
BF16 = jnp.bfloat16

ROWS1, ROWS2 = 512, 1792


def leaky(values):
    root = lax.rsqrt(values * values + 1.0)
    return 0.6 * values + 0.4 * ((values * values + 1.0) * root - 1.0)


def leaky_slope(values):
    return 0.6 + 0.4 * values * lax.rsqrt(values * values + 1.0)


def dot_nt(lhs, rhs):
    return lax.dot_general(lhs, rhs, (((1,), (1,)), ((), ())), preferred_element_type=F32)


def dot_tn(lhs, rhs):
    return lax.dot_general(lhs, rhs, (((0,), (0,)), ((), ())), preferred_element_type=F32)


def dot_nn(lhs, rhs):
    return lax.dot_general(lhs, rhs, (((1,), (0,)), ((), ())), preferred_element_type=F32)


def window(ref, *lead):
    low = ref[lead + (pl.ds(0, 8),)].reshape(256, 128)
    high = ref[lead + (pl.ds(1, 8),)].reshape(256, 128)
    return jnp.concatenate([low, high], axis=1)


def make_kernel(n_dep, n_row, n_col):
    n_half = n_row // 2
    n_plane = n_dep * n_half

    def kernel(
        vol_in, w1_in, w2_in, cot_in, g1_out, g2_out,
        vol, w1, w2, cot, load_sem,
        s_ref, f_ref, w1f, w1b, w2b, up,
        f_sc, f_sr, f_sk, f_c, f_r, f_d, f_dc, f_dr, f_drc,
        hs, hx, slope1, h_sc, h_sr, h_sd, h_sk, h_c, h_r, h_d, h_dc, h_dr, h_drc,
        q_ref, dx, g1acc, q_sc, q_sr, q_sd, q_sk, q_c, q_r, q_rc, q_d, q_dc, q_dr, q_drc,
        acc1, swap1, send1, come1, cols1, gath1, full1,
        acc2, swap2, send2, come2, cols2, gath2,
        halo_send, halo_recv, sum_send1, sum_recv1, sum_send2, sum_recv2,
    ):
        dep, row, col = lax.axis_index("depth"), lax.axis_index("row"), lax.axis_index("col")
        core, line = lax.rem(row, 2), lax.div(row, 2)
        plane = dep * n_half + line

        loads = [
            pltpu.make_async_copy(src, dst, load_sem.at[i])
            for i, (src, dst) in enumerate(((vol_in, vol), (w1_in, w1), (w2_in, w2), (cot_in, cot)))
        ]
        for load in loads:
            load.start()

        def plane_dev(index):
            return (lax.div(index, n_half), 2 * lax.rem(index, n_half) + core, col)

        def shifted(step, d, r, c):
            return (
                lax.rem(dep + d * step + n_dep, n_dep),
                lax.rem(row + r * step + n_row, n_row),
                lax.rem(col + c * step + n_col, n_col),
            )

        mate = (dep, row + 1 - 2 * core, col)
        corners = [(d, r, c) for d in (0, 1) for r in (0, 1) for c in (0, 1)][1:]

        barrier = pltpu.get_barrier_semaphore()
        peers = [shifted(s, *e) for e in corners for s in (1, -1)]
        peers.append(mate)
        peers += [plane_dev(lax.rem(plane + s, n_plane)) for s in range(1, n_plane)]
        peers += [(dep, row, lax.rem(col + s, n_col)) for s in range(1, n_col)]
        for peer in peers:
            pl.semaphore_signal(barrier, inc=1, device_id=peer, device_id_type=MESH)

        loads[0].wait()
        for rd in range(4):
            for t in (7, 0, 1, 2, 3, 4, 5, 6):
                s_ref[rd, 1 + t, pl.ds(24, 128), :] = (
                    vol[:, rd, :, pl.ds(128 * t, 128)].astype(F32).reshape(128, 128)
                )
        for t in range(8):
            rows = [s_ref[rd, 1 + t, pl.ds(24 + 15, 8, stride=16), :] for rd in range(4)]
            f_sr[t] = jnp.concatenate(rows, axis=0).astype(BF16)
        lane = lax.broadcasted_iota(jnp.int32, (128, 128), 1)
        packed = s_ref[3, 8, pl.ds(24, 128), :]
        for rd in range(3):
            moved = pltpu.roll(s_ref[rd, 8, pl.ds(24, 128), :], 32 * rd + 32, 1)
            packed = jnp.where((lane >= 32 * rd) & (lane < 32 * rd + 32), moved, packed)
        f_sc[...] = packed.astype(BF16)
        for t in range(8):
            f_sk[pl.ds(t, 1), :] = s_ref[3, 1 + t, pl.ds(151, 1), :]

        pl.semaphore_wait(barrier, len(peers))

        def halo(phase, kind, src, dst, step):
            index = phase * 7 + kind
            return pltpu.make_async_remote_copy(
                src_ref=src, dst_ref=dst, send_sem=halo_send.at[index], recv_sem=halo_recv.at[index],
                device_id=shifted(step, *corners[kind]), device_id_type=MESH,
            )

        field_copies = [
            halo(0, 6, f_sc.at[pl.ds(112, 16)], f_drc, 1),
            halo(0, 5, f_sk, f_dr, 1),
            halo(0, 4, f_sc.at[pl.ds(112, 16)], f_dc, 1),
            halo(0, 3, vol.at[7, 3], f_d, 1),
            halo(0, 2, f_sr.at[7], f_r.at[0], 1),
            halo(0, 1, f_sr, f_r.at[pl.ds(1, 8)], 1),
            halo(0, 0, f_sc, f_c, 1),
        ]
        for copy in field_copies:
            copy.start()

        for load in loads[1:]:
            load.wait()
        w1f[:, pl.ds(768, 128)] = jnp.zeros((64, 128), F32)
        w1f[:, pl.ds(0, 864)] = w1[...].astype(F32)
        lane1 = lax.broadcasted_iota(jnp.int32, (64, 256), 1)
        for ab in range(9):
            tile, off = divmod(ab * 96, 128)
            if tile == 6:
                band = jnp.concatenate([w1f[:, pl.ds(768, 128)], jnp.zeros((64, 128), F32)], axis=1)
            else:
                band = w1f[:, pl.ds(128 * tile, 256)]
            for kk, start in ((0, 96), (1, 160)):
                moved = pltpu.roll(band, (start - off) % 256, 1)
                keep = (lane1 >= start) & (lane1 < start + 96)
                w1b[ab, pl.ds(64 * kk, 64), :] = jnp.where(keep, moved, 0.0).astype(BF16)
            w2b[ab, pl.ds(0, 64), :] = jnp.zeros((64, 128), BF16)
            w2b[ab, pl.ds(64, 192), :] = w2[pl.ds(192 * ab, 192), :]
        for i in range(8):
            line_up = cot[i].astype(F32)
            for k in range(8):
                up[k, pl.ds(4 * i, 4), :] = line_up[:, 128 * k : 128 * (k + 1)]

        def pick_field(t, rd, rr):
            source, start = (3, 8) if rd < 0 else (rd, 24)
            rows = s_ref[source, t, pl.ds(start + rr, 32, stride=4), :]
            f_ref[rd + 1, rr + 1, t] = rows.astype(BF16)

        def local_tile(t, carry):
            for rd in range(4):
                for rr in range(4):
                    pick_field(t, rd, rr)
            return carry

        lax.fori_loop(1, 9, local_tile, 0)

        first_dep, first_row, first_col = dep == 0, row == 0, col == 0

        def unless(edge, values):
            return jnp.where(edge, 0.0, values.astype(F32))

        def first_section(pd, pr):
            pre = jnp.zeros((256, 128), F32)
            for ab in range(9):
                a, b = divmod(ab, 3)
                pre += dot_nt(window(f_ref, 2 * pd + a, 2 * pr + b), w1b[ab])
            hid = leaky(pre).reshape(8, 32, 128)
            hs[pd, pr, pl.ds(1, 8), pl.ds(8, 32), :] = hid
            slope1[pd, pr] = leaky_slope(pre)
            h_sc[2 * pd + pr] = hid[7].astype(BF16)

        hidden_copies = [
            halo(1, 6, h_sk, h_drc, 1),
            halo(1, 5, h_sk, h_dr, 1),
            halo(1, 1, h_sr, h_r.at[pl.ds(1, 8)], 1),
            halo(1, 2, h_sr.at[7], h_r.at[0], 1),
            halo(1, 3, h_sd, h_d, 1),
            halo(1, 4, h_sd.at[3], h_dc, 1),
            halo(1, 0, h_sc, h_c, 1),
        ]
        field_copies[6].wait_recv()
        packed = unless(first_col, f_c[...])
        for rd in range(4):
            s_ref[rd, 0, pl.ds(24, 128), :] = packed if rd == 3 else pltpu.roll(packed, 96 - 32 * rd, 1)
        for rd in range(4):
            for rr in range(4):
                pick_field(0, rd, rr)
        first_section(1, 1)
        for t in range(8):
            h_sk[pl.ds(t, 1), :] = hs[1, 1, 1 + t, pl.ds(39, 1), :]
        for copy in hidden_copies[:2]:
            copy.start()

        field_copies[2].wait_recv()
        field_copies[3].wait_recv()
        for t in range(8):
            s_ref[3, 1 + t, pl.ds(8, 16), :] = unless(first_dep, f_d[:, pl.ds(128 * t, 128)])
        s_ref[3, 0, pl.ds(8, 16), :] = unless(first_dep | first_col, f_dc[...])

        def above_tile(t, carry):
            for rr in range(4):
                pick_field(t, -1, rr)
            return carry

        lax.fori_loop(0, 9, above_tile, 0)
        first_section(0, 1)
        for t in range(8):
            rows = [hs[pd, 1, 1 + t, pl.ds(11, 8, stride=4), :] for pd in range(2)]
            h_sr[t] = jnp.concatenate(rows, axis=0).astype(BF16)
        for copy in hidden_copies[2:4]:
            copy.start()

        field_copies[4].wait_recv()
        field_copies[5].wait_recv()

        def row_tile(t, carry):
            block = unless(first_row | (first_col & (t == 0)), f_r[t])
            for rd in range(4):
                s_ref[rd, t, pl.ds(23, 8, stride=16), :] = block[8 * rd : 8 * rd + 8]
            for rd in range(4):
                pick_field(t, rd, -1)
            return carry

        lax.fori_loop(0, 9, row_tile, 0)
        first_section(1, 0)
        for t in range(4):
            rows = [hs[1, pr, 1 + 2 * t + u, pl.ds(36, 4), :] for u in range(2) for pr in range(2)]
            h_sd[t] = jnp.concatenate(rows, axis=0).astype(BF16)
        for copy in hidden_copies[4:6]:
            copy.start()

        field_copies[0].wait_recv()
        field_copies[1].wait_recv()
        s_ref[3, 0, pl.ds(7, 1), :] = unless(first_dep | first_row | first_col, f_drc[...])[15:16]
        block = unless(first_dep | first_row, f_dr[...])
        for t in range(8):
            s_ref[3, 1 + t, pl.ds(7, 1), :] = block[t : t + 1]

        def edge_tile(t, carry):
            pick_field(t, -1, -1)
            return carry

        lax.fori_loop(0, 9, edge_tile, 0)
        first_section(0, 0)
        hidden_copies[6].start()

        def pick_hidden(a, b, pd, pr, start):
            hx[3 * a + b] = hs[pd, pr, :, pl.ds(start, 32), :].astype(BF16)

        for copy in hidden_copies:
            copy.wait_recv()
        for pd in range(2):
            for pr in range(2):
                hs[pd, pr, 0, pl.ds(8, 32), :] = unless(first_col, h_c[2 * pd + pr])
        for t in range(4):
            block = unless(first_dep, h_d[t])
            for u in range(2):
                for pr in range(2):
                    start = 8 * u + 4 * pr
                    hs[1, pr, 1 + 2 * t + u, pl.ds(4, 4), :] = block[start : start + 4]
        block = unless(first_dep | first_col, h_dc[...])
        for pr in range(2):
            hs[1, pr, 0, pl.ds(4, 4), :] = block[8 + 4 * pr : 12 + 4 * pr]
        for pr in range(2):
            pick_hidden(0, 1 + pr, 1, pr, 4)
            pick_hidden(1, 1 + pr, 0, pr, 8)
            pick_hidden(2, 1 + pr, 1, pr, 8)
        for t in range(9):
            edge = first_row | first_col if t == 0 else first_row
            block = unless(edge, h_r[t])
            for pd in range(2):
                hs[pd, 1, t, pl.ds(7, 8, stride=4), :] = block[8 * pd : 8 * pd + 8]
        block = unless(first_dep | first_row, h_dr[...])
        for t in range(8):
            hs[1, 1, 1 + t, pl.ds(3, 1), :] = block[t : t + 1]
        hs[1, 1, 0, pl.ds(3, 1), :] = unless(first_dep | first_row | first_col, h_drc[...])[7:8]
        pick_hidden(0, 0, 1, 1, 3)
        pick_hidden(1, 0, 0, 1, 7)
        pick_hidden(2, 0, 1, 1, 7)

        pre = jnp.zeros((256, 128), F32)
        for ab in range(9):
            pre += dot_nn(window(hx, ab), w2b[ab])
        delta2 = up[...].reshape(256, 128) * leaky_slope(pre)
        q_ref[pl.ds(0, 8), pl.ds(0, 32), :] = delta2.reshape(8, 32, 128)
        q_sc[...] = delta2[:32].astype(BF16)
        for t in range(4):
            rows = [q_ref[2 * t + u, pl.ds(0, 8, stride=4), :] for u in range(2)]
            q_sr[t] = jnp.concatenate(rows, axis=0).astype(BF16)
            rows = [q_ref[2 * t + u, pl.ds(0, 8), :] for u in range(2)]
            q_sd[t] = jnp.concatenate(rows, axis=0).astype(BF16)
        for t in range(8):
            q_sk[pl.ds(t, 1), :] = q_ref[t, pl.ds(0, 1), :]
        delta_copies = [
            halo(2, 6, q_sd.at[0], q_drc, -1),
            halo(2, 5, q_sk, q_dr, -1),
            halo(2, 4, q_sd.at[0], q_dc, -1),
            halo(2, 3, q_sd, q_d, -1),
            halo(2, 2, q_sr.at[0], q_rc, -1),
            halo(2, 1, q_sr, q_r, -1),
            halo(2, 0, q_sc, q_c, -1),
        ]
        for copy in delta_copies:
            copy.start()

        def summing(rows, acc, swap, send, come, cols, gath, sems_out, sems_in):
            half, chunk = rows // 2, rows // (2 * n_plane)

            def remote(index, src, dst, dev):
                return pltpu.make_async_remote_copy(
                    src_ref=src, dst_ref=dst, send_sem=sems_out.at[index], recv_sem=sems_in.at[index],
                    device_id=dev, device_id_type=MESH,
                )

            order = sorted(range(1, n_plane), key=lambda s: -min(s % n_half, n_half - s % n_half))
            other = pl.multiple_of((1 - core) * half, 8)
            mine = pl.multiple_of(core * half, 8)
            first = remote(0, acc.at[pl.ds(other, half)], swap, mate)
            spread, around, back, onward = {}, {}, {}, {}
            own = gath.at[core, plane]
            for s in order:
                target = lax.rem(plane + s, n_plane)
                spread[s] = remote(s, send.at[target], come.at[s], plane_dev(target))
                back[s] = remote(n_plane + s, own, own, plane_dev(target))
                came = gath.at[core, lax.rem(plane - s + n_plane, n_plane)]
                onward[s] = remote(2 * n_plane + s, came, came, mate)
            onward[0] = remote(2 * n_plane, own, own, mate)
            for s in range(1, n_col):
                target = lax.rem(col + s, n_col)
                around[s] = remote(3 * n_plane + s, cols.at[col], cols.at[col], (dep, row, target))

            def to_plane():
                first.wait_recv()
                summed = acc[pl.ds(mine, half), :] + swap[...]
                send[...] = summed.reshape(n_plane, chunk, 128).astype(BF16)
                for s in order:
                    spread[s].start()

            def to_column():
                place = pl.multiple_of(plane * chunk, 8)
                total = acc[pl.ds(mine + place, chunk), :] + swap[pl.ds(place, chunk), :]
                for s in reversed(order):
                    spread[s].wait_recv()
                    total += come[s].astype(F32)
                cols[col] = total.astype(BF16)
                for s in sorted(around, key=lambda s: -min(s, n_col - s)):
                    around[s].start()

            def to_all():
                for s in around:
                    around[s].wait_recv()
                total = cols[0].astype(F32)
                for k in range(1, n_col):
                    total += cols[k].astype(F32)
                gath[core, plane] = total.astype(BF16)
                for s in order:
                    back[s].start()
                onward[0].start()

            def to_mate():
                for s in reversed(order):
                    back[s].wait_recv()
                    onward[s].start()

            def finish():
                for s in onward:
                    onward[s].wait_recv()

            def drain():
                first.wait_send()
                for group in (spread, around, back, onward):
                    for s in group:
                        group[s].wait_send()

            return first.start, to_plane, to_column, to_all, to_mate, finish, drain

        sum1 = summing(ROWS1, acc1, swap1, send1, come1, cols1, gath1, sum_send1, sum_recv1)
        sum2 = summing(ROWS2, acc2, swap2, send2, come2, cols2, gath2, sum_send2, sum_recv2)

        flat2 = delta2.astype(BF16)
        for ab in range(9):
            acc2[pl.ds(192 * ab, 192), :] = dot_tn(window(hx, ab), flat2)[64:]
        acc2[pl.ds(1728, 64), :] = jnp.zeros((64, 128), F32)
        sum2[0]()
        sum2[1]()

        last_dep, last_row, last_col = dep == n_dep - 1, row == n_row - 1, col == n_col - 1
        taps = (((1, 0),), ((2, 0), (0, 1)))

        def way_back(pd, pr):
            back = jnp.zeros((256, 128), F32)
            for a, od in taps[pd]:
                for b, o_r in taps[pr]:
                    band = jnp.concatenate(
                        [w2b[3 * a + b, pl.ds(128, 128), :], w2b[3 * a + b, pl.ds(0, 128), :]], axis=1
                    )
                    back += dot_nt(window(dx, 2 * od + o_r), band)
            delta1 = (back * slope1[pd, pr]).T.astype(BF16)
            for ab in range(9):
                a, b = divmod(ab, 3)
                grad = dot_nn(delta1, window(f_ref, 2 * pd + a, 2 * pr + b))
                if pd + pr > 0:
                    grad += g1acc[ab]
                if pd + pr < 2:
                    g1acc[ab] = grad
                else:
                    yield grad

        delta_copies[6].wait_recv()
        q_ref[8, pl.ds(0, 32), :] = unless(last_col, q_c[...])
        dx[0] = q_ref[:, pl.ds(0, 32), :].astype(BF16)
        list(way_back(0, 0))
        delta_copies[2].wait_recv()
        delta_copies[3].wait_recv()
        for t in range(8):
            u = 8 * (t % 2)
            q_ref[t, pl.ds(32, 4), :] = unless(last_dep, q_d[t // 2])[u : u + 4]
        q_ref[8, pl.ds(32, 4), :] = unless(last_dep | last_col, q_dc[...])[:4]
        dx[2] = q_ref[:, pl.ds(4, 32), :].astype(BF16)
        list(way_back(1, 0))
        delta_copies[4].wait_recv()
        delta_copies[5].wait_recv()
        for t in range(8):
            u = 8 * (t % 2)
            q_ref[t, pl.ds(4, 8, stride=4), :] = unless(last_row, q_r[t // 2])[u : u + 8]
        q_ref[8, pl.ds(4, 8, stride=4), :] = unless(last_row | last_col, q_rc[...])[:8]
        dx[1] = q_ref[:, pl.ds(1, 32), :].astype(BF16)
        list(way_back(0, 1))
        delta_copies[0].wait_recv()
        delta_copies[1].wait_recv()
        block = unless(last_dep | last_row, q_dr[...])
        for t in range(8):
            q_ref[t, pl.ds(36, 1), :] = block[t : t + 1]
        q_ref[8, pl.ds(36, 1), :] = unless(last_dep | last_row | last_col, q_drc[...])[:1]
        dx[3] = q_ref[:, pl.ds(5, 32), :].astype(BF16)

        lane = lax.broadcasted_iota(jnp.int32, (64, 256), 1)
        tiles = [jnp.zeros((64, 128), F32) for _ in range(8)]
        for ab, grad in enumerate(way_back(1, 1)):
            both = grad[:64] + pltpu.roll(grad[64:], 256 - 64, 1)
            both = jnp.where((lane >= 96) & (lane < 192), both, 0.0)
            tile, off = divmod(ab * 96, 128)
            both = pltpu.roll(both, (off - 96) % 256, 1)
            tiles[tile] = tiles[tile] + both[:, :128]
            tiles[tile + 1] = tiles[tile + 1] + both[:, 128:]
        for t in range(8):
            acc1[pl.ds(64 * t, 64), :] = tiles[t]

        sum1[0]()
        sum1[1]()
        sum2[2]()
        sum1[2]()
        sum2[3]()
        sum1[3]()
        sum2[4]()
        sum1[4]()
        sum2[5]()
        chunk1, chunk2 = ROWS1 // (2 * n_plane), ROWS2 // (2 * n_plane)
        for h in range(2):
            for w in range(n_plane):
                start = (h * n_plane + w) * chunk2
                size = min(chunk2, 1728 - start)
                if size > 0:
                    g2_out[pl.ds(start, size), :] = gath2[h, w].astype(F32)[:size]
        sum1[5]()
        for h in range(2):
            for w in range(n_plane):
                full1[pl.ds((h * n_plane + w) * chunk1, chunk1), :] = gath1[h, w].astype(F32)
        for t in range(6):
            g1_out[:, pl.ds(128 * t, 128)] = full1[pl.ds(64 * t, 64), :]
        g1_out[:, pl.ds(768, 96)] = full1[pl.ds(384, 64), pl.ds(0, 96)]
        sum1[6]()
        sum2[6]()
        for copy in field_copies + hidden_copies + delta_copies:
            copy.wait_send()

    return kernel


def write_out(g1_in, g2_in, g1_out, g2_out, sems):
    second = pltpu.make_async_copy(g2_in, g2_out, sems.at[1])
    second.start()
    first = pltpu.make_async_copy(g1_in, g1_out, sems.at[0])
    first.start()
    first.wait()
    second.wait()


def solution(mesh):
    n_dep, n_row, n_col = mesh.shape["depth"], mesh.shape["row"], mesh.shape["col"]
    n_plane = n_dep * n_row // 2
    kernel = make_kernel(n_dep, n_row, n_col)
    n_sum = 3 * n_plane + n_col

    def vm(shape, dtype):
        return pltpu.VMEM(shape, dtype)

    def sum_scratch(rows):
        half, chunk = rows // 2, rows // (2 * n_plane)
        return [
            vm((rows, 128), F32), vm((half, 128), F32),
            vm((n_plane, chunk, 128), BF16), vm((n_plane, chunk, 128), BF16),
            vm((n_col, chunk, 128), BF16), vm((2, n_plane, chunk, 128), BF16),
        ]

    def shards(volume, first_weight, second_weight, cotangent):
        first_grad, second_grad = pl.pallas_call(
            kernel,
            out_shape=(
                jax.ShapeDtypeStruct((64, 864), F32),
                jax.ShapeDtypeStruct((1728, 128), F32),
            ),
            in_specs=[pl.BlockSpec(memory_space=pltpu.HBM)] * 4,
            out_specs=(pl.BlockSpec(memory_space=pltpu.VMEM),) * 2,
            scratch_shapes=[
                vm((8, 4, 16, 1024), BF16), vm((64, 864), BF16), vm((1728, 128), BF16), vm((8, 4, 1024), BF16),
                pltpu.SemaphoreType.DMA((4,)),
                vm((4, 9, 152, 128), F32), vm((5, 5, 9, 32, 128), BF16),
                vm((64, 896), F32), vm((9, 128, 256), BF16), vm((9, 256, 128), BF16), vm((8, 32, 128), F32),
                vm((128, 128), BF16), vm((8, 32, 128), BF16), vm((8, 128), F32),
                vm((128, 128), BF16), vm((9, 32, 128), BF16), vm((16, 1024), BF16), vm((16, 128), BF16),
                vm((8, 128), F32), vm((16, 128), BF16),
                vm((2, 2, 9, 40, 128), F32), vm((9, 9, 32, 128), BF16), vm((2, 2, 256, 128), F32),
                vm((4, 32, 128), BF16), vm((8, 16, 128), BF16), vm((4, 16, 128), BF16), vm((8, 128), F32),
                vm((4, 32, 128), BF16), vm((9, 16, 128), BF16), vm((4, 16, 128), BF16), vm((16, 128), BF16),
                vm((8, 128), F32), vm((8, 128), F32),
                vm((9, 40, 128), F32), vm((4, 9, 32, 128), BF16), vm((9, 128, 256), F32),
                vm((32, 128), BF16), vm((4, 16, 128), BF16), vm((4, 16, 128), BF16), vm((8, 128), F32),
                vm((32, 128), BF16), vm((4, 16, 128), BF16), vm((16, 128), BF16),
                vm((4, 16, 128), BF16), vm((16, 128), BF16), vm((8, 128), F32), vm((16, 128), BF16),
                *sum_scratch(ROWS1), vm((ROWS1, 128), F32), *sum_scratch(ROWS2),
                pltpu.SemaphoreType.DMA((21,)), pltpu.SemaphoreType.DMA((21,)),
                pltpu.SemaphoreType.DMA((n_sum,)), pltpu.SemaphoreType.DMA((n_sum,)),
                pltpu.SemaphoreType.DMA((n_sum,)), pltpu.SemaphoreType.DMA((n_sum,)),
            ],
            compiler_params=pltpu.CompilerParams(
                collective_id=0, has_side_effects=True, vmem_limit_bytes=48 * 1024 * 1024
            ),
            name="sections",
        )(*[
            pltpu.with_memory_space_constraint(x, pltpu.HBM)
            for x in (volume.reshape(8, 4, 16, 1024), first_weight, second_weight.T, cotangent)
        ])
        first_grad, second_grad = pl.pallas_call(
            write_out,
            out_shape=(
                jax.ShapeDtypeStruct((64, 864), F32),
                jax.ShapeDtypeStruct((1728, 128), F32),
            ),
            in_specs=[pl.BlockSpec(memory_space=pltpu.VMEM)] * 2,
            out_specs=(pl.BlockSpec(memory_space=pltpu.HBM),) * 2,
            scratch_shapes=[pltpu.SemaphoreType.DMA((2,))],
            name="write_out",
        )(pltpu.with_memory_space_constraint(first_grad, pltpu.VMEM), pltpu.with_memory_space_constraint(second_grad, pltpu.VMEM))
        return first_grad, second_grad.T

    placed = (P("depth", "row", "col"), P(), P(), P("depth", "row", "col"))
    return jax.shard_map(shards, mesh=mesh, in_specs=placed, out_specs=(P(), P()), check_vma=False)
```

```python
import jax
import jax.numpy as jnp
from jax import lax
from jax.experimental import pallas as pl
from jax.experimental.pallas import tpu as pltpu
from jax.sharding import PartitionSpec as P

MESH = pl.DeviceIdType.MESH
F32 = jnp.float32
BF16 = jnp.bfloat16

ROWS1, ROWS2 = 512, 1792


def leaky(values):
    root = lax.rsqrt(values * values + 1.0)
    return 0.6 * values + 0.4 * ((values * values + 1.0) * root - 1.0)


def leaky_slope(values):
    return 0.6 + 0.4 * values * lax.rsqrt(values * values + 1.0)


def dot_nt(lhs, rhs):
    return lax.dot_general(lhs, rhs, (((1,), (1,)), ((), ())), preferred_element_type=F32)


def dot_tn(lhs, rhs):
    return lax.dot_general(lhs, rhs, (((0,), (0,)), ((), ())), preferred_element_type=F32)


def dot_nn(lhs, rhs):
    return lax.dot_general(lhs, rhs, (((1,), (0,)), ((), ())), preferred_element_type=F32)


def window(ref, *lead):
    low = ref[lead + (pl.ds(0, 8),)].reshape(256, 128)
    high = ref[lead + (pl.ds(1, 8),)].reshape(256, 128)
    return jnp.concatenate([low, high], axis=1)


def make_kernel(n_dep, n_row, n_col):
    n_half = n_row // 2
    n_plane = n_dep * n_half

    def kernel(
        vol_in, w1_in, w2_in, cot_in, g1_out, g2_out,
        vol, w1, w2, cot, load_sem,
        s_ref, f_ref, w1f, w1b, w2b, up,
        f_sc, f_sr, f_sk, f_c, f_r, f_d, f_dc, f_dr, f_drc,
        hs, hx, slope1, h_sc, h_sr, h_sd, h_sk, h_c, h_r, h_d, h_dc, h_dr, h_drc,
        q_ref, dx, g1acc, q_sc, q_sr, q_sd, q_sk, q_c, q_r, q_rc, q_d, q_dc, q_dr, q_drc,
        acc1, swap1, send1, come1, cols1, gath1, full1,
        acc2, swap2, send2, come2, cols2, gath2,
        halo_send, halo_recv, sum_send1, sum_recv1, sum_send2, sum_recv2,
    ):
        dep, row, col = lax.axis_index("depth"), lax.axis_index("row"), lax.axis_index("col")
        core, line = lax.rem(row, 2), lax.div(row, 2)
        plane = dep * n_half + line

        loads = [
            pltpu.make_async_copy(src, dst, load_sem.at[i])
            for i, (src, dst) in enumerate(((vol_in, vol), (w1_in, w1), (w2_in, w2), (cot_in, cot)))
        ]
        loads[0].start()

        def plane_dev(index):
            return (lax.div(index, n_half), 2 * lax.rem(index, n_half) + core, col)

        def shifted(step, d, r, c):
            return (
                lax.rem(dep + d * step + n_dep, n_dep),
                lax.rem(row + r * step + n_row, n_row),
                lax.rem(col + c * step + n_col, n_col),
            )

        mate = (dep, row + 1 - 2 * core, col)
        corners = [(d, r, c) for d in (0, 1) for r in (0, 1) for c in (0, 1)][1:]

        barrier = pltpu.get_barrier_semaphore()
        peers = [shifted(s, *e) for e in corners for s in (1, -1)]
        peers.append(mate)
        peers += [plane_dev(lax.rem(plane + s, n_plane)) for s in range(1, n_plane)]
        peers += [(dep, row, lax.rem(col + s, n_col)) for s in range(1, n_col)]
        for peer in peers:
            pl.semaphore_signal(barrier, inc=1, device_id=peer, device_id_type=MESH)
        for load in loads[1:]:
            load.start()

        loads[0].wait()
        for rd in range(4):
            for t in (7, 0, 1, 2, 3, 4, 5, 6):
                s_ref[rd, 1 + t, pl.ds(24, 128), :] = (
                    vol[:, rd, :, pl.ds(128 * t, 128)].astype(F32).reshape(128, 128)
                )
        for t in range(8):
            rows = [s_ref[rd, 1 + t, pl.ds(24 + 15, 8, stride=16), :] for rd in range(4)]
            f_sr[t] = jnp.concatenate(rows, axis=0).astype(BF16)
        lane = lax.broadcasted_iota(jnp.int32, (128, 128), 1)
        packed = s_ref[3, 8, pl.ds(24, 128), :]
        for rd in range(3):
            moved = pltpu.roll(s_ref[rd, 8, pl.ds(24, 128), :], 32 * rd + 32, 1)
            packed = jnp.where((lane >= 32 * rd) & (lane < 32 * rd + 32), moved, packed)
        f_sc[...] = packed.astype(BF16)
        for t in range(8):
            f_sk[pl.ds(t, 1), :] = s_ref[3, 1 + t, pl.ds(151, 1), :]

        pl.semaphore_wait(barrier, len(peers))

        def halo(phase, kind, src, dst, step):
            index = phase * 7 + kind
            return pltpu.make_async_remote_copy(
                src_ref=src, dst_ref=dst, send_sem=halo_send.at[index], recv_sem=halo_recv.at[index],
                device_id=shifted(step, *corners[kind]), device_id_type=MESH,
            )

        field_copies = [
            halo(0, 6, f_sc.at[pl.ds(112, 16)], f_drc, 1),
            halo(0, 5, f_sk, f_dr, 1),
            halo(0, 4, f_sc.at[pl.ds(112, 16)], f_dc, 1),
            halo(0, 3, vol.at[7, 3], f_d, 1),
            halo(0, 2, f_sr.at[7], f_r.at[0], 1),
            halo(0, 1, f_sr, f_r.at[pl.ds(1, 8)], 1),
            halo(0, 0, f_sc, f_c, 1),
        ]
        for copy in field_copies:
            copy.start()

        for load in loads[1:]:
            load.wait()
        w1f[:, pl.ds(768, 128)] = jnp.zeros((64, 128), F32)
        w1f[:, pl.ds(0, 864)] = w1[...].astype(F32)
        lane1 = lax.broadcasted_iota(jnp.int32, (64, 256), 1)
        for ab in range(9):
            tile, off = divmod(ab * 96, 128)
            if tile == 6:
                band = jnp.concatenate([w1f[:, pl.ds(768, 128)], jnp.zeros((64, 128), F32)], axis=1)
            else:
                band = w1f[:, pl.ds(128 * tile, 256)]
            for kk, start in ((0, 96), (1, 160)):
                moved = pltpu.roll(band, (start - off) % 256, 1)
                keep = (lane1 >= start) & (lane1 < start + 96)
                w1b[ab, pl.ds(64 * kk, 64), :] = jnp.where(keep, moved, 0.0).astype(BF16)
            w2b[ab, pl.ds(0, 64), :] = jnp.zeros((64, 128), BF16)
            w2b[ab, pl.ds(64, 192), :] = w2[pl.ds(192 * ab, 192), :]
        for i in range(8):
            line_up = cot[i].astype(F32)
            for k in range(8):
                up[k, pl.ds(4 * i, 4), :] = line_up[:, 128 * k : 128 * (k + 1)]

        def pick_field(t, rd, rr):
            source, start = (3, 8) if rd < 0 else (rd, 24)
            rows = s_ref[source, t, pl.ds(start + rr, 32, stride=4), :]
            f_ref[rd + 1, rr + 1, t] = rows.astype(BF16)

        def local_tile(t, carry):
            for rd in range(4):
                for rr in range(4):
                    pick_field(t, rd, rr)
            return carry

        lax.fori_loop(1, 9, local_tile, 0)

        for rd in range(4):
            for rr in range(4):
                f_ref[rd + 1, rr + 1, 0] = jnp.zeros((32, 128), BF16)

        def tap_places(pd, pr, local):
            for ab in range(9):
                place = (2 * pd + ab // 3, 2 * pr + ab % 3)
                if (min(place) > 0) == local:
                    yield ab, place

        for pd in range(2):
            for pr in range(2):
                pre = jnp.zeros((256, 128), F32)
                for ab, place in tap_places(pd, pr, True):
                    pre += dot_nt(window(f_ref, *place), w1b[ab])
                slope1[pd, pr] = pre

        first_dep, first_row, first_col = dep == 0, row == 0, col == 0

        def unless(edge, values):
            return jnp.where(edge, 0.0, values.astype(F32))

        def first_section(pd, pr):
            edge = jnp.zeros((32, 128), F32)
            for ab, place in tap_places(pd, pr, True):
                edge += dot_nt(f_ref[place + (0,)], w1b[ab, :, pl.ds(0, 128)])
            pre = slope1[pd, pr]
            pre = jnp.concatenate([pre[:32] + edge, pre[32:]], axis=0)
            for ab, place in tap_places(pd, pr, False):
                pre += dot_nt(window(f_ref, *place), w1b[ab])
            hid = leaky(pre).reshape(8, 32, 128)
            hs[pd, pr, pl.ds(1, 8), pl.ds(8, 32), :] = hid
            slope1[pd, pr] = leaky_slope(pre)
            h_sc[2 * pd + pr] = hid[7].astype(BF16)

        hidden_copies = [
            halo(1, 6, h_sk, h_drc, 1),
            halo(1, 5, h_sk, h_dr, 1),
            halo(1, 1, h_sr, h_r.at[pl.ds(1, 8)], 1),
            halo(1, 2, h_sr.at[7], h_r.at[0], 1),
            halo(1, 3, h_sd, h_d, 1),
            halo(1, 4, h_sd.at[3], h_dc, 1),
            halo(1, 0, h_sc, h_c, 1),
        ]
        field_copies[6].wait_recv()
        packed = unless(first_col, f_c[...])
        for rd in range(4):
            s_ref[rd, 0, pl.ds(24, 128), :] = packed if rd == 3 else pltpu.roll(packed, 96 - 32 * rd, 1)
        for rd in range(4):
            for rr in range(4):
                pick_field(0, rd, rr)
        first_section(1, 1)
        for t in range(8):
            h_sk[pl.ds(t, 1), :] = hs[1, 1, 1 + t, pl.ds(39, 1), :]
        for copy in hidden_copies[:2]:
            copy.start()

        field_copies[2].wait_recv()
        field_copies[3].wait_recv()
        for t in range(8):
            s_ref[3, 1 + t, pl.ds(8, 16), :] = unless(first_dep, f_d[:, pl.ds(128 * t, 128)])
        s_ref[3, 0, pl.ds(8, 16), :] = unless(first_dep | first_col, f_dc[...])

        def above_tile(t, carry):
            for rr in range(4):
                pick_field(t, -1, rr)
            return carry

        lax.fori_loop(0, 9, above_tile, 0)
        first_section(0, 1)
        for t in range(8):
            rows = [hs[pd, 1, 1 + t, pl.ds(11, 8, stride=4), :] for pd in range(2)]
            h_sr[t] = jnp.concatenate(rows, axis=0).astype(BF16)
        for copy in hidden_copies[2:4]:
            copy.start()

        field_copies[4].wait_recv()
        field_copies[5].wait_recv()

        def row_tile(t, carry):
            block = unless(first_row | (first_col & (t == 0)), f_r[t])
            for rd in range(4):
                s_ref[rd, t, pl.ds(23, 8, stride=16), :] = block[8 * rd : 8 * rd + 8]
            for rd in range(4):
                pick_field(t, rd, -1)
            return carry

        lax.fori_loop(0, 9, row_tile, 0)
        first_section(1, 0)
        for t in range(4):
            rows = [hs[1, pr, 1 + 2 * t + u, pl.ds(36, 4), :] for u in range(2) for pr in range(2)]
            h_sd[t] = jnp.concatenate(rows, axis=0).astype(BF16)
        for copy in hidden_copies[4:6]:
            copy.start()

        field_copies[0].wait_recv()
        field_copies[1].wait_recv()
        s_ref[3, 0, pl.ds(7, 1), :] = unless(first_dep | first_row | first_col, f_drc[...])[15:16]
        block = unless(first_dep | first_row, f_dr[...])
        for t in range(8):
            s_ref[3, 1 + t, pl.ds(7, 1), :] = block[t : t + 1]

        def edge_tile(t, carry):
            pick_field(t, -1, -1)
            return carry

        lax.fori_loop(0, 9, edge_tile, 0)
        first_section(0, 0)
        hidden_copies[6].start()

        def pick_hidden(a, b, pd, pr, start):
            hx[3 * a + b] = hs[pd, pr, :, pl.ds(start, 32), :].astype(BF16)

        for copy in hidden_copies:
            copy.wait_recv()
        for pd in range(2):
            for pr in range(2):
                hs[pd, pr, 0, pl.ds(8, 32), :] = unless(first_col, h_c[2 * pd + pr])
        for t in range(4):
            block = unless(first_dep, h_d[t])
            for u in range(2):
                for pr in range(2):
                    start = 8 * u + 4 * pr
                    hs[1, pr, 1 + 2 * t + u, pl.ds(4, 4), :] = block[start : start + 4]
        block = unless(first_dep | first_col, h_dc[...])
        for pr in range(2):
            hs[1, pr, 0, pl.ds(4, 4), :] = block[8 + 4 * pr : 12 + 4 * pr]
        for pr in range(2):
            pick_hidden(0, 1 + pr, 1, pr, 4)
            pick_hidden(1, 1 + pr, 0, pr, 8)
            pick_hidden(2, 1 + pr, 1, pr, 8)
        for t in range(9):
            edge = first_row | first_col if t == 0 else first_row
            block = unless(edge, h_r[t])
            for pd in range(2):
                hs[pd, 1, t, pl.ds(7, 8, stride=4), :] = block[8 * pd : 8 * pd + 8]
        block = unless(first_dep | first_row, h_dr[...])
        for t in range(8):
            hs[1, 1, 1 + t, pl.ds(3, 1), :] = block[t : t + 1]
        hs[1, 1, 0, pl.ds(3, 1), :] = unless(first_dep | first_row | first_col, h_drc[...])[7:8]
        pick_hidden(0, 0, 1, 1, 3)
        pick_hidden(1, 0, 0, 1, 7)
        pick_hidden(2, 0, 1, 1, 7)

        pre = jnp.zeros((256, 128), F32)
        for ab in range(9):
            pre += dot_nn(window(hx, ab), w2b[ab])
        delta2 = up[...].reshape(256, 128) * leaky_slope(pre)
        q_ref[pl.ds(0, 8), pl.ds(0, 32), :] = delta2.reshape(8, 32, 128)
        q_sc[...] = delta2[:32].astype(BF16)
        for t in range(4):
            rows = [q_ref[2 * t + u, pl.ds(0, 8, stride=4), :] for u in range(2)]
            q_sr[t] = jnp.concatenate(rows, axis=0).astype(BF16)
            rows = [q_ref[2 * t + u, pl.ds(0, 8), :] for u in range(2)]
            q_sd[t] = jnp.concatenate(rows, axis=0).astype(BF16)
        for t in range(8):
            q_sk[pl.ds(t, 1), :] = q_ref[t, pl.ds(0, 1), :]
        delta_copies = [
            halo(2, 6, q_sd.at[0], q_drc, -1),
            halo(2, 5, q_sk, q_dr, -1),
            halo(2, 4, q_sd.at[0], q_dc, -1),
            halo(2, 3, q_sd, q_d, -1),
            halo(2, 2, q_sr.at[0], q_rc, -1),
            halo(2, 1, q_sr, q_r, -1),
            halo(2, 0, q_sc, q_c, -1),
        ]
        for copy in delta_copies:
            copy.start()

        def summing(rows, acc, swap, send, come, cols, gath, sems_out, sems_in, cuts):
            half, chunk = rows // 2, rows // (2 * n_plane)

            def remote(index, src, dst, dev):
                return pltpu.make_async_remote_copy(
                    src_ref=src, dst_ref=dst, send_sem=sems_out.at[index], recv_sem=sems_in.at[index],
                    device_id=dev, device_id_type=MESH,
                )

            order = sorted(range(1, n_plane), key=lambda s: -min(s % n_half, n_half - s % n_half))
            pieces = [(low, high) for low, high in zip((0,) + cuts, cuts + (n_plane,)) if high > low]
            first = []
            for i, (low, high) in enumerate(pieces):
                part = pl.ds(low * chunk, (high - low) * chunk)
                first.append(remote(3 * n_plane + n_col + i, acc.at[1 - core, part], swap.at[part], mate))
            spread, around, back, onward = {}, {}, {}, {}
            own = gath.at[core, plane]
            for s in order:
                target = lax.rem(plane + s, n_plane)
                spread[s] = remote(s, send.at[target], come.at[s], plane_dev(target))
                back[s] = remote(n_plane + s, own, own, plane_dev(target))
                came = gath.at[core, lax.rem(plane - s + n_plane, n_plane)]
                onward[s] = remote(2 * n_plane + s, came, came, mate)
            onward[0] = remote(2 * n_plane, own, own, mate)
            for s in range(1, n_col):
                target = lax.rem(col + s, n_col)
                around[s] = remote(3 * n_plane + s, cols.at[col], cols.at[col], (dep, row, target))

            def to_plane():
                for (low, high), copy in zip(pieces, first):
                    copy.wait_recv()
                    part = pl.ds(low * chunk, (high - low) * chunk)
                    summed = acc[core, part, :] + swap[part, :]
                    send[pl.ds(low, high - low)] = summed.reshape(high - low, chunk, 128).astype(BF16)
                for s in order:
                    spread[s].start()

            def to_column():
                place = pl.multiple_of(plane * chunk, 8)
                total = acc[core, pl.ds(place, chunk), :] + swap[pl.ds(place, chunk), :]
                for s in reversed(order):
                    spread[s].wait_recv()
                    total += come[s].astype(F32)
                cols[col] = total.astype(BF16)
                for s in sorted(around, key=lambda s: -min(s, n_col - s)):
                    around[s].start()

            def to_all():
                for s in around:
                    around[s].wait_recv()
                total = cols[0].astype(F32)
                for k in range(1, n_col):
                    total += cols[k].astype(F32)
                gath[core, plane] = total.astype(BF16)
                for s in order:
                    back[s].start()
                onward[0].start()

            def to_mate():
                for s in reversed(order):
                    back[s].wait_recv()
                    onward[s].start()

            def finish():
                for s in onward:
                    onward[s].wait_recv()

            def drain(*names):
                for name in names:
                    group = {"first": dict(enumerate(first)), "spread": spread, "around": around, "back": back, "onward": onward}[name]
                    for s in group:
                        group[s].wait_send()

            return list(first), to_plane, to_column, to_all, to_mate, finish, drain

        sum1 = summing(ROWS1, acc1, swap1, send1, come1, cols1, gath1, sum_send1, sum_recv1, ())
        chunk2 = ROWS2 // (2 * n_plane)
        sum2 = summing(ROWS2, acc2, swap2, send2, come2, cols2, gath2, sum_send2, sum_recv2, (288 // chunk2, 576 // chunk2))

        flat2 = delta2.astype(BF16)
        acc2[:, pl.ds(864, 32), :] = jnp.zeros((2, 32, 128), F32)
        ready = 0
        for ab in range(9):
            grad = dot_tn(window(hx, ab), flat2)
            for h in range(2):
                acc2[h, pl.ds(96 * ab, 96), :] = grad[64 + 96 * h : 160 + 96 * h]
            if ab % 3 == 2:
                whole = n_plane if ab == 8 else 96 * (ab + 1) // chunk2
                if whole > ready:
                    sum2[0].pop(0).start()
                ready = whole
        sum2[1]()

        last_dep, last_row, last_col = dep == n_dep - 1, row == n_row - 1, col == n_col - 1
        taps = (((1, 0),), ((2, 0), (0, 1)))

        def way_back(pd, pr):
            back = jnp.zeros((256, 128), F32)
            for a, od in taps[pd]:
                for b, o_r in taps[pr]:
                    band = jnp.concatenate(
                        [w2b[3 * a + b, pl.ds(128, 128), :], w2b[3 * a + b, pl.ds(0, 128), :]], axis=1
                    )
                    back += dot_nt(window(dx, 2 * od + o_r), band)
            delta1 = (back * slope1[pd, pr]).T.astype(BF16)
            for ab in range(9):
                a, b = divmod(ab, 3)
                grad = dot_nn(delta1, window(f_ref, 2 * pd + a, 2 * pr + b))
                if pd + pr > 0:
                    grad += g1acc[ab]
                if pd + pr < 2:
                    g1acc[ab] = grad
                else:
                    yield grad

        delta_copies[6].wait_recv()
        q_ref[8, pl.ds(0, 32), :] = unless(last_col, q_c[...])
        dx[0] = q_ref[:, pl.ds(0, 32), :].astype(BF16)
        list(way_back(0, 0))
        delta_copies[2].wait_recv()
        delta_copies[3].wait_recv()
        for t in range(8):
            u = 8 * (t % 2)
            q_ref[t, pl.ds(32, 4), :] = unless(last_dep, q_d[t // 2])[u : u + 4]
        q_ref[8, pl.ds(32, 4), :] = unless(last_dep | last_col, q_dc[...])[:4]
        dx[2] = q_ref[:, pl.ds(4, 32), :].astype(BF16)
        list(way_back(1, 0))
        delta_copies[4].wait_recv()
        delta_copies[5].wait_recv()
        for t in range(8):
            u = 8 * (t % 2)
            q_ref[t, pl.ds(4, 8, stride=4), :] = unless(last_row, q_r[t // 2])[u : u + 8]
        q_ref[8, pl.ds(4, 8, stride=4), :] = unless(last_row | last_col, q_rc[...])[:8]
        dx[1] = q_ref[:, pl.ds(1, 32), :].astype(BF16)
        list(way_back(0, 1))
        delta_copies[0].wait_recv()
        delta_copies[1].wait_recv()
        block = unless(last_dep | last_row, q_dr[...])
        for t in range(8):
            q_ref[t, pl.ds(36, 1), :] = block[t : t + 1]
        q_ref[8, pl.ds(36, 1), :] = unless(last_dep | last_row | last_col, q_drc[...])[:1]
        dx[3] = q_ref[:, pl.ds(5, 32), :].astype(BF16)

        lane = lax.broadcasted_iota(jnp.int32, (64, 256), 1)
        tiles = [jnp.zeros((64, 128), F32) for _ in range(8)]
        for ab, grad in enumerate(way_back(1, 1)):
            both = grad[:64] + pltpu.roll(grad[64:], 256 - 64, 1)
            both = jnp.where((lane >= 96) & (lane < 192), both, 0.0)
            tile, off = divmod(ab * 96, 128)
            both = pltpu.roll(both, (off - 96) % 256, 1)
            tiles[tile] = tiles[tile] + both[:, :128]
            tiles[tile + 1] = tiles[tile + 1] + both[:, 128:]
        for t in range(8):
            acc1[t // 4, pl.ds(64 * (t % 4), 64), :] = tiles[t]

        def widen2(h):
            for w in range(n_plane):
                row = w * chunk2
                values = gath2[h, w].astype(F32)
                while row < min((w + 1) * chunk2, 864):
                    stop = min((row // 96 + 1) * 96, (w + 1) * chunk2, 864)
                    start = pl.multiple_of(row // 96 * 192 + row % 96 + h * 96, 8)
                    g2_out[pl.ds(start, stop - row), :] = values[row - w * chunk2 : stop - w * chunk2]
                    row = stop

        sum1[0][0].start()
        for copy in field_copies + hidden_copies + delta_copies:
            copy.wait_send()
        sum1[1]()
        sum2[2]()
        sum1[6]("first")
        sum2[6]("first", "spread")
        sum1[2]()
        sum1[6]("spread")
        sum2[3]()
        sum2[6]("around")
        sum1[3]()
        sum1[6]("around")
        sum2[4]()
        widen2(core)
        sum2[6]("back")
        sum1[4]()
        sum2[5]()
        sum2[6]("onward")
        widen2(1 - core)

        def widen(h):
            start = pl.multiple_of(h * (ROWS1 // 2), 8)
            full1[pl.ds(start, ROWS1 // 2), :] = gath1[h].astype(F32).reshape(ROWS1 // 2, 128)

        widen(core)
        sum1[6]("back")
        sum1[5]()
        widen(1 - core)
        for t in range(6):
            g1_out[:, pl.ds(128 * t, 128)] = full1[pl.ds(64 * t, 64), :]
        g1_out[:, pl.ds(768, 96)] = full1[pl.ds(384, 64), pl.ds(0, 96)]
        sum1[6]("onward")

    return kernel


def write_out(g1_in, g2_in, g1_out, g2_out, sems):
    second = pltpu.make_async_copy(g2_in, g2_out, sems.at[1])
    second.start()
    first = pltpu.make_async_copy(g1_in, g1_out, sems.at[0])
    first.start()
    first.wait()
    second.wait()


def solution(mesh):
    n_dep, n_row, n_col = mesh.shape["depth"], mesh.shape["row"], mesh.shape["col"]
    n_plane = n_dep * n_row // 2
    kernel = make_kernel(n_dep, n_row, n_col)
    n_sum = 3 * n_plane + n_col + 3

    def vm(shape, dtype):
        return pltpu.VMEM(shape, dtype)

    def sum_scratch(rows):
        half, chunk = rows // 2, rows // (2 * n_plane)
        return [
            vm((2, half, 128), F32), vm((half, 128), F32),
            vm((n_plane, chunk, 128), BF16), vm((n_plane, chunk, 128), BF16),
            vm((n_col, chunk, 128), BF16), vm((2, n_plane, chunk, 128), BF16),
        ]

    def shards(volume, first_weight, second_weight, cotangent):
        first_grad, second_grad = pl.pallas_call(
            kernel,
            out_shape=(
                jax.ShapeDtypeStruct((64, 864), F32),
                jax.ShapeDtypeStruct((1728, 128), F32),
            ),
            in_specs=[pl.BlockSpec(memory_space=pltpu.HBM)] * 4,
            out_specs=(pl.BlockSpec(memory_space=pltpu.VMEM),) * 2,
            scratch_shapes=[
                vm((8, 4, 16, 1024), BF16), vm((64, 864), BF16), vm((1728, 128), BF16), vm((8, 4, 1024), BF16),
                pltpu.SemaphoreType.DMA((4,)),
                vm((4, 9, 152, 128), F32), vm((5, 5, 9, 32, 128), BF16),
                vm((64, 896), F32), vm((9, 128, 256), BF16), vm((9, 256, 128), BF16), vm((8, 32, 128), F32),
                vm((128, 128), BF16), vm((8, 32, 128), BF16), vm((8, 128), F32),
                vm((128, 128), BF16), vm((9, 32, 128), BF16), vm((16, 1024), BF16), vm((16, 128), BF16),
                vm((8, 128), F32), vm((16, 128), BF16),
                vm((2, 2, 9, 40, 128), F32), vm((9, 9, 32, 128), BF16), vm((2, 2, 256, 128), F32),
                vm((4, 32, 128), BF16), vm((8, 16, 128), BF16), vm((4, 16, 128), BF16), vm((8, 128), F32),
                vm((4, 32, 128), BF16), vm((9, 16, 128), BF16), vm((4, 16, 128), BF16), vm((16, 128), BF16),
                vm((8, 128), F32), vm((8, 128), F32),
                vm((9, 40, 128), F32), vm((4, 9, 32, 128), BF16), vm((9, 128, 256), F32),
                vm((32, 128), BF16), vm((4, 16, 128), BF16), vm((4, 16, 128), BF16), vm((8, 128), F32),
                vm((32, 128), BF16), vm((4, 16, 128), BF16), vm((16, 128), BF16),
                vm((4, 16, 128), BF16), vm((16, 128), BF16), vm((8, 128), F32), vm((16, 128), BF16),
                *sum_scratch(ROWS1), vm((ROWS1, 128), F32), *sum_scratch(ROWS2),
                pltpu.SemaphoreType.DMA((21,)), pltpu.SemaphoreType.DMA((21,)),
                pltpu.SemaphoreType.DMA((n_sum,)), pltpu.SemaphoreType.DMA((n_sum,)),
                pltpu.SemaphoreType.DMA((n_sum,)), pltpu.SemaphoreType.DMA((n_sum,)),
            ],
            compiler_params=pltpu.CompilerParams(
                collective_id=0, has_side_effects=True, vmem_limit_bytes=48 * 1024 * 1024
            ),
            name="sections",
        )(*[
            pltpu.with_memory_space_constraint(x, pltpu.HBM)
            for x in (volume.reshape(8, 4, 16, 1024), first_weight, second_weight.T, cotangent)
        ])
        first_grad, second_grad = pl.pallas_call(
            write_out,
            out_shape=(
                jax.ShapeDtypeStruct((64, 864), F32),
                jax.ShapeDtypeStruct((1728, 128), F32),
            ),
            in_specs=[pl.BlockSpec(memory_space=pltpu.VMEM)] * 2,
            out_specs=(pl.BlockSpec(memory_space=pltpu.HBM),) * 2,
            scratch_shapes=[pltpu.SemaphoreType.DMA((2,))],
            name="write_out",
        )(pltpu.with_memory_space_constraint(first_grad, pltpu.VMEM), pltpu.with_memory_space_constraint(second_grad, pltpu.VMEM))
        return first_grad, second_grad.T

    placed = (P("depth", "row", "col"), P(), P(), P("depth", "row", "col"))
    return jax.shard_map(shards, mesh=mesh, in_specs=placed, out_specs=(P(), P()), check_vma=False)
```

```python
import jax
import jax.numpy as jnp
from jax import lax
from jax.experimental import pallas as pl
from jax.experimental.pallas import tpu as pltpu
from jax.sharding import PartitionSpec as P

MESH = pl.DeviceIdType.MESH
F32 = jnp.float32
BF16 = jnp.bfloat16

ROWS1, ROWS2 = 512, 1792


def leaky(values):
    root = lax.rsqrt(values * values + 1.0)
    return 0.6 * values + 0.4 * ((values * values + 1.0) * root - 1.0)


def leaky_slope(values):
    return 0.6 + 0.4 * values * lax.rsqrt(values * values + 1.0)


def dot_nt(lhs, rhs):
    return lax.dot_general(lhs, rhs, (((1,), (1,)), ((), ())), preferred_element_type=F32)


def dot_tn(lhs, rhs):
    return lax.dot_general(lhs, rhs, (((0,), (0,)), ((), ())), preferred_element_type=F32)


def dot_nn(lhs, rhs):
    return lax.dot_general(lhs, rhs, (((1,), (0,)), ((), ())), preferred_element_type=F32)


def window(ref, *lead):
    low = ref[lead + (pl.ds(0, 8),)].reshape(256, 128)
    high = ref[lead + (pl.ds(1, 8),)].reshape(256, 128)
    return jnp.concatenate([low, high], axis=1)


def make_kernel(n_dep, n_row, n_col):
    n_half = n_row // 2
    n_plane = n_dep * n_half

    def kernel(
        vol_in, w1_in, w2_in, cot_in, g1_out, g2_out,
        vol, w1, w2, cot, load_sem,
        s_ref, f_ref, w1f, w1b, w2b, up,
        f_sc, f_sr, f_sk, f_c, f_r, f_d, f_dc, f_dr, f_drc,
        hs, hx, slope1, h_sc, h_sr, h_sd, h_sk, h_c, h_r, h_d, h_dc, h_dr, h_drc,
        q_ref, dx, g1acc, q_sc, q_sr, q_sd, q_sk, q_c, q_r, q_rc, q_d, q_dc, q_dr, q_drc,
        acc1, swap1, send1, come1, cols1, gath1, full1,
        acc2, swap2, send2, come2, cols2, gath2,
        halo_send, halo_recv, sum_send1, sum_recv1, sum_send2, sum_recv2,
    ):
        dep, row, col = lax.axis_index("depth"), lax.axis_index("row"), lax.axis_index("col")
        core, line = lax.rem(row, 2), lax.div(row, 2)
        plane = dep * n_half + line

        loads = [
            pltpu.make_async_copy(src, dst, load_sem.at[i])
            for i, (src, dst) in enumerate(((vol_in, vol), (w1_in, w1), (w2_in, w2), (cot_in, cot)))
        ]
        loads[0].start()

        def plane_dev(index):
            return (lax.div(index, n_half), 2 * lax.rem(index, n_half) + core, col)

        def shifted(step, d, r, c):
            return (
                lax.rem(dep + d * step + n_dep, n_dep),
                lax.rem(row + r * step + n_row, n_row),
                lax.rem(col + c * step + n_col, n_col),
            )

        mate = (dep, row + 1 - 2 * core, col)
        corners = [(d, r, c) for d in (0, 1) for r in (0, 1) for c in (0, 1)][1:]

        barrier = pltpu.get_barrier_semaphore()
        peers = [shifted(s, *e) for e in corners for s in (1, -1)]
        peers.append(mate)
        peers += [plane_dev(lax.rem(plane + s, n_plane)) for s in range(1, n_plane)]
        peers += [(dep, row, lax.rem(col + s, n_col)) for s in range(1, n_col)]
        for peer in peers:
            pl.semaphore_signal(barrier, inc=1, device_id=peer, device_id_type=MESH)
        for load in loads[1:]:
            load.start()

        loads[0].wait()
        for rd in range(4):
            for t in (7, 0, 1, 2, 3, 4, 5, 6):
                s_ref[rd, 1 + t, pl.ds(24, 128), :] = (
                    vol[:, rd, :, pl.ds(128 * t, 128)].astype(F32).reshape(128, 128)
                )
        for t in range(8):
            rows = [s_ref[rd, 1 + t, pl.ds(24 + 15, 8, stride=16), :] for rd in range(4)]
            f_sr[t] = jnp.concatenate(rows, axis=0).astype(BF16)
        lane = lax.broadcasted_iota(jnp.int32, (128, 128), 1)
        packed = s_ref[3, 8, pl.ds(24, 128), :]
        for rd in range(3):
            moved = pltpu.roll(s_ref[rd, 8, pl.ds(24, 128), :], 32 * rd + 32, 1)
            packed = jnp.where((lane >= 32 * rd) & (lane < 32 * rd + 32), moved, packed)
        f_sc[...] = packed.astype(BF16)
        for t in range(8):
            f_sk[pl.ds(t, 1), :] = s_ref[3, 1 + t, pl.ds(151, 1), :]

        pl.semaphore_wait(barrier, len(peers))

        def halo(phase, kind, src, dst, step, index=None):
            index = phase * 7 + kind if index is None else index
            return pltpu.make_async_remote_copy(
                src_ref=src, dst_ref=dst, send_sem=halo_send.at[index], recv_sem=halo_recv.at[index],
                device_id=shifted(step, *corners[kind]), device_id_type=MESH,
            )

        field_copies = [
            halo(0, 6, f_sc.at[pl.ds(112, 16)], f_drc, 1),
            halo(0, 5, f_sk, f_dr, 1),
            halo(0, 4, f_sc.at[pl.ds(112, 16)], f_dc, 1),
            halo(0, 3, vol.at[7, 3], f_d, 1),
            halo(0, 2, f_sr.at[7], f_r.at[0], 1),
            halo(0, 1, f_sr, f_r.at[pl.ds(1, 8)], 1),
            halo(0, 0, f_sc, f_c, 1),
        ]
        for copy in field_copies:
            copy.start()

        for load in loads[1:]:
            load.wait()
        w1f[:, pl.ds(768, 128)] = jnp.zeros((64, 128), F32)
        w1f[:, pl.ds(0, 864)] = w1[...].astype(F32)
        lane1 = lax.broadcasted_iota(jnp.int32, (64, 256), 1)
        for ab in range(9):
            tile, off = divmod(ab * 96, 128)
            if tile == 6:
                band = jnp.concatenate([w1f[:, pl.ds(768, 128)], jnp.zeros((64, 128), F32)], axis=1)
            else:
                band = w1f[:, pl.ds(128 * tile, 256)]
            for kk, start in ((0, 96), (1, 160)):
                moved = pltpu.roll(band, (start - off) % 256, 1)
                keep = (lane1 >= start) & (lane1 < start + 96)
                w1b[ab, pl.ds(64 * kk, 64), :] = jnp.where(keep, moved, 0.0).astype(BF16)
            w2b[ab, pl.ds(0, 64), :] = jnp.zeros((64, 128), BF16)
            w2b[ab, pl.ds(64, 192), :] = w2[pl.ds(192 * ab, 192), :]
        for i in range(8):
            line_up = cot[i].astype(F32)
            for k in range(8):
                up[k, pl.ds(4 * i, 4), :] = line_up[:, 128 * k : 128 * (k + 1)]

        def pick_field(t, rd, rr):
            source, start = (3, 8) if rd < 0 else (rd, 24)
            rows = s_ref[source, t, pl.ds(start + rr, 32, stride=4), :]
            f_ref[rd + 1, rr + 1, t] = rows.astype(BF16)

        def local_tile(t, carry):
            for rd in range(4):
                for rr in range(4):
                    pick_field(t, rd, rr)
            return carry

        lax.fori_loop(1, 9, local_tile, 0)

        for rd in range(4):
            for rr in range(4):
                f_ref[rd + 1, rr + 1, 0] = jnp.zeros((32, 128), BF16)

        def tap_places(pd, pr, local):
            for ab in range(9):
                place = (2 * pd + ab // 3, 2 * pr + ab % 3)
                if (min(place) > 0) == local:
                    yield ab, place

        for pd in range(2):
            for pr in range(2):
                pre = jnp.zeros((256, 128), F32)
                for ab, place in tap_places(pd, pr, True):
                    pre += dot_nt(window(f_ref, *place), w1b[ab])
                slope1[pd, pr] = pre

        first_dep, first_row, first_col = dep == 0, row == 0, col == 0

        def unless(edge, values):
            return jnp.where(edge, 0.0, values.astype(F32))

        def first_section(pd, pr):
            edge = jnp.zeros((32, 128), F32)
            for ab, place in tap_places(pd, pr, True):
                edge += dot_nt(f_ref[place + (0,)], w1b[ab, :, pl.ds(0, 128)])
            pre = slope1[pd, pr]
            pre = jnp.concatenate([pre[:32] + edge, pre[32:]], axis=0)
            for ab, place in tap_places(pd, pr, False):
                pre += dot_nt(window(f_ref, *place), w1b[ab])
            hid = leaky(pre).reshape(8, 32, 128)
            hs[pd, pr, pl.ds(1, 8), pl.ds(8, 32), :] = hid
            slope1[pd, pr] = leaky_slope(pre)
            h_sc[2 * pd + pr] = hid[7].astype(BF16)

        hidden_copies = [
            halo(1, 6, h_sk, h_drc, 1),
            halo(1, 5, h_sk, h_dr, 1),
            halo(1, 1, h_sr, h_r.at[pl.ds(1, 8)], 1),
            halo(1, 2, h_sr.at[7], h_r.at[0], 1),
            halo(1, 3, h_sd, h_d, 1),
            halo(1, 4, h_sd.at[3], h_dc, 1),
            halo(1, 0, h_sc.at[3], h_c.at[3], 1),
            halo(1, 0, h_sc.at[1], h_c.at[1], 1, 21),
            halo(1, 0, h_sc.at[2], h_c.at[2], 1, 22),
            halo(1, 0, h_sc.at[0], h_c.at[0], 1, 23),
        ]
        field_copies[6].wait_recv()
        packed = unless(first_col, f_c[...])
        for rd in range(4):
            s_ref[rd, 0, pl.ds(24, 128), :] = packed if rd == 3 else pltpu.roll(packed, 96 - 32 * rd, 1)
        for rd in range(4):
            for rr in range(4):
                pick_field(0, rd, rr)
        first_section(1, 1)
        for t in range(8):
            h_sk[pl.ds(t, 1), :] = hs[1, 1, 1 + t, pl.ds(39, 1), :]
        for copy in hidden_copies[:2] + hidden_copies[6:7]:
            copy.start()

        field_copies[2].wait_recv()
        field_copies[3].wait_recv()
        for t in range(8):
            s_ref[3, 1 + t, pl.ds(8, 16), :] = unless(first_dep, f_d[:, pl.ds(128 * t, 128)])
        s_ref[3, 0, pl.ds(8, 16), :] = unless(first_dep | first_col, f_dc[...])

        def above_tile(t, carry):
            for rr in range(4):
                pick_field(t, -1, rr)
            return carry

        lax.fori_loop(0, 9, above_tile, 0)
        first_section(0, 1)
        for t in range(8):
            rows = [hs[pd, 1, 1 + t, pl.ds(11, 8, stride=4), :] for pd in range(2)]
            h_sr[t] = jnp.concatenate(rows, axis=0).astype(BF16)
        for copy in hidden_copies[2:4] + hidden_copies[7:8]:
            copy.start()

        field_copies[4].wait_recv()
        field_copies[5].wait_recv()

        def row_tile(t, carry):
            block = unless(first_row | (first_col & (t == 0)), f_r[t])
            for rd in range(4):
                s_ref[rd, t, pl.ds(23, 8, stride=16), :] = block[8 * rd : 8 * rd + 8]
            for rd in range(4):
                pick_field(t, rd, -1)
            return carry

        lax.fori_loop(0, 9, row_tile, 0)
        first_section(1, 0)
        for t in range(4):
            rows = [hs[1, pr, 1 + 2 * t + u, pl.ds(36, 4), :] for u in range(2) for pr in range(2)]
            h_sd[t] = jnp.concatenate(rows, axis=0).astype(BF16)
        for copy in hidden_copies[4:6] + hidden_copies[8:9]:
            copy.start()

        field_copies[0].wait_recv()
        field_copies[1].wait_recv()
        s_ref[3, 0, pl.ds(7, 1), :] = unless(first_dep | first_row | first_col, f_drc[...])[15:16]
        block = unless(first_dep | first_row, f_dr[...])
        for t in range(8):
            s_ref[3, 1 + t, pl.ds(7, 1), :] = block[t : t + 1]

        def edge_tile(t, carry):
            pick_field(t, -1, -1)
            return carry

        lax.fori_loop(0, 9, edge_tile, 0)
        first_section(0, 0)
        hidden_copies[9].start()

        def pick_hidden(a, b, pd, pr, start):
            hx[3 * a + b] = hs[pd, pr, :, pl.ds(start, 32), :].astype(BF16)

        for copy in hidden_copies:
            copy.wait_recv()
        for pd in range(2):
            for pr in range(2):
                hs[pd, pr, 0, pl.ds(8, 32), :] = unless(first_col, h_c[2 * pd + pr])
        for t in range(4):
            block = unless(first_dep, h_d[t])
            for u in range(2):
                for pr in range(2):
                    start = 8 * u + 4 * pr
                    hs[1, pr, 1 + 2 * t + u, pl.ds(4, 4), :] = block[start : start + 4]
        block = unless(first_dep | first_col, h_dc[...])
        for pr in range(2):
            hs[1, pr, 0, pl.ds(4, 4), :] = block[8 + 4 * pr : 12 + 4 * pr]
        for pr in range(2):
            pick_hidden(0, 1 + pr, 1, pr, 4)
            pick_hidden(1, 1 + pr, 0, pr, 8)
            pick_hidden(2, 1 + pr, 1, pr, 8)
        for t in range(9):
            edge = first_row | first_col if t == 0 else first_row
            block = unless(edge, h_r[t])
            for pd in range(2):
                hs[pd, 1, t, pl.ds(7, 8, stride=4), :] = block[8 * pd : 8 * pd + 8]
        block = unless(first_dep | first_row, h_dr[...])
        for t in range(8):
            hs[1, 1, 1 + t, pl.ds(3, 1), :] = block[t : t + 1]
        hs[1, 1, 0, pl.ds(3, 1), :] = unless(first_dep | first_row | first_col, h_drc[...])[7:8]
        pick_hidden(0, 0, 1, 1, 3)
        pick_hidden(1, 0, 0, 1, 7)
        pick_hidden(2, 0, 1, 1, 7)

        pre = jnp.zeros((256, 128), F32)
        for ab in range(9):
            pre += dot_nn(window(hx, ab), w2b[ab])
        delta2 = up[...].reshape(256, 128) * leaky_slope(pre)
        q_ref[pl.ds(0, 8), pl.ds(0, 32), :] = delta2.reshape(8, 32, 128)
        q_sc[...] = delta2[:32].astype(BF16)
        for t in range(4):
            rows = [q_ref[2 * t + u, pl.ds(0, 8, stride=4), :] for u in range(2)]
            q_sr[t] = jnp.concatenate(rows, axis=0).astype(BF16)
            rows = [q_ref[2 * t + u, pl.ds(0, 8), :] for u in range(2)]
            q_sd[t] = jnp.concatenate(rows, axis=0).astype(BF16)
        for t in range(8):
            q_sk[pl.ds(t, 1), :] = q_ref[t, pl.ds(0, 1), :]
        delta_copies = [
            halo(2, 6, q_sd.at[0], q_drc, -1),
            halo(2, 5, q_sk, q_dr, -1),
            halo(2, 4, q_sd.at[0], q_dc, -1),
            halo(2, 3, q_sd, q_d, -1),
            halo(2, 2, q_sr.at[0], q_rc, -1),
            halo(2, 1, q_sr, q_r, -1),
            halo(2, 0, q_sc, q_c, -1),
        ]
        for copy in reversed(delta_copies):
            copy.start()

        def summing(rows, acc, swap, send, come, cols, gath, sems_out, sems_in, cuts):
            half, chunk = rows // 2, rows // (2 * n_plane)

            def remote(index, src, dst, dev):
                return pltpu.make_async_remote_copy(
                    src_ref=src, dst_ref=dst, send_sem=sems_out.at[index], recv_sem=sems_in.at[index],
                    device_id=dev, device_id_type=MESH,
                )

            order = sorted(range(1, n_plane), key=lambda s: -min(s % n_half, n_half - s % n_half))
            pieces = [(low, high) for low, high in zip((0,) + cuts, cuts + (n_plane,)) if high > low]
            first = []
            for i, (low, high) in enumerate(pieces):
                part = pl.ds(low * chunk, (high - low) * chunk)
                first.append(remote(3 * n_plane + n_col + i, acc.at[1 - core, part], swap.at[part], mate))
            spread, around, back, onward = {}, {}, {}, {}
            own = gath.at[core, plane]
            for s in order:
                target = lax.rem(plane + s, n_plane)
                spread[s] = remote(s, send.at[target], come.at[s], plane_dev(target))
                back[s] = remote(n_plane + s, own, own, plane_dev(target))
                came = gath.at[core, lax.rem(plane - s + n_plane, n_plane)]
                onward[s] = remote(2 * n_plane + s, came, came, mate)
            onward[0] = remote(2 * n_plane, own, own, mate)
            for s in range(1, n_col):
                target = lax.rem(col + s, n_col)
                around[s] = remote(3 * n_plane + s, cols.at[col], cols.at[col], (dep, row, target))

            def to_plane():
                for (low, high), copy in zip(pieces, first):
                    copy.wait_recv()
                    part = pl.ds(low * chunk, (high - low) * chunk)
                    summed = acc[core, part, :] + swap[part, :]
                    send[pl.ds(low, high - low)] = summed.reshape(high - low, chunk, 128).astype(BF16)
                for s in order:
                    spread[s].start()

            def to_column():
                place = pl.multiple_of(plane * chunk, 8)
                total = acc[core, pl.ds(place, chunk), :] + swap[pl.ds(place, chunk), :]
                for s in reversed(order):
                    spread[s].wait_recv()
                    total += come[s].astype(F32)
                cols[col] = total.astype(BF16)
                for s in sorted(around, key=lambda s: -min(s, n_col - s)):
                    around[s].start()

            def to_all():
                for s in around:
                    around[s].wait_recv()
                total = cols[0].astype(F32)
                for k in range(1, n_col):
                    total += cols[k].astype(F32)
                gath[core, plane] = total.astype(BF16)
                for s in order:
                    back[s].start()
                onward[0].start()

            def to_mate():
                for s in reversed(order):
                    back[s].wait_recv()
                    onward[s].start()

            def finish():
                for s in onward:
                    onward[s].wait_recv()

            def drain(*names):
                for name in names:
                    group = {"first": dict(enumerate(first)), "spread": spread, "around": around, "back": back, "onward": onward}[name]
                    for s in group:
                        group[s].wait_send()

            return list(first), to_plane, to_column, to_all, to_mate, finish, drain

        sum1 = summing(ROWS1, acc1, swap1, send1, come1, cols1, gath1, sum_send1, sum_recv1, ())
        chunk2 = ROWS2 // (2 * n_plane)
        sum2 = summing(ROWS2, acc2, swap2, send2, come2, cols2, gath2, sum_send2, sum_recv2, (288 // chunk2, 576 // chunk2))

        flat2 = delta2.astype(BF16)
        acc2[:, pl.ds(864, 32), :] = jnp.zeros((2, 32, 128), F32)
        ready = 0
        for ab in range(9):
            grad = dot_tn(window(hx, ab), flat2)
            for h in range(2):
                acc2[h, pl.ds(96 * ab, 96), :] = grad[64 + 96 * h : 160 + 96 * h]
            if ab % 3 == 2:
                whole = n_plane if ab == 8 else 96 * (ab + 1) // chunk2
                if whole > ready:
                    sum2[0].pop(0).start()
                ready = whole
        sum2[1]()

        last_dep, last_row, last_col = dep == n_dep - 1, row == n_row - 1, col == n_col - 1
        taps = (((1, 0),), ((2, 0), (0, 1)))

        def way_back(pd, pr):
            back = jnp.zeros((256, 128), F32)
            for a, od in taps[pd]:
                for b, o_r in taps[pr]:
                    band = jnp.concatenate(
                        [w2b[3 * a + b, pl.ds(128, 128), :], w2b[3 * a + b, pl.ds(0, 128), :]], axis=1
                    )
                    back += dot_nt(window(dx, 2 * od + o_r), band)
            delta1 = (back * slope1[pd, pr]).T.astype(BF16)
            for ab in range(9):
                a, b = divmod(ab, 3)
                grad = dot_nn(delta1, window(f_ref, 2 * pd + a, 2 * pr + b))
                if pd + pr > 0:
                    grad += g1acc[ab]
                if pd + pr < 2:
                    g1acc[ab] = grad
                else:
                    yield grad

        delta_copies[6].wait_recv()
        q_ref[8, pl.ds(0, 32), :] = unless(last_col, q_c[...])
        dx[0] = q_ref[:, pl.ds(0, 32), :].astype(BF16)
        list(way_back(0, 0))
        delta_copies[2].wait_recv()
        delta_copies[3].wait_recv()
        for t in range(8):
            u = 8 * (t % 2)
            q_ref[t, pl.ds(32, 4), :] = unless(last_dep, q_d[t // 2])[u : u + 4]
        q_ref[8, pl.ds(32, 4), :] = unless(last_dep | last_col, q_dc[...])[:4]
        dx[2] = q_ref[:, pl.ds(4, 32), :].astype(BF16)
        list(way_back(1, 0))
        delta_copies[4].wait_recv()
        delta_copies[5].wait_recv()
        for t in range(8):
            u = 8 * (t % 2)
            q_ref[t, pl.ds(4, 8, stride=4), :] = unless(last_row, q_r[t // 2])[u : u + 8]
        q_ref[8, pl.ds(4, 8, stride=4), :] = unless(last_row | last_col, q_rc[...])[:8]
        dx[1] = q_ref[:, pl.ds(1, 32), :].astype(BF16)
        list(way_back(0, 1))
        delta_copies[0].wait_recv()
        delta_copies[1].wait_recv()
        block = unless(last_dep | last_row, q_dr[...])
        for t in range(8):
            q_ref[t, pl.ds(36, 1), :] = block[t : t + 1]
        q_ref[8, pl.ds(36, 1), :] = unless(last_dep | last_row | last_col, q_drc[...])[:1]
        dx[3] = q_ref[:, pl.ds(5, 32), :].astype(BF16)

        lane = lax.broadcasted_iota(jnp.int32, (64, 256), 1)
        tiles = [jnp.zeros((64, 128), F32) for _ in range(8)]
        for ab, grad in enumerate(way_back(1, 1)):
            both = grad[:64] + pltpu.roll(grad[64:], 256 - 64, 1)
            both = jnp.where((lane >= 96) & (lane < 192), both, 0.0)
            tile, off = divmod(ab * 96, 128)
            both = pltpu.roll(both, (off - 96) % 256, 1)
            tiles[tile] = tiles[tile] + both[:, :128]
            tiles[tile + 1] = tiles[tile + 1] + both[:, 128:]
        for t in range(8):
            acc1[t // 4, pl.ds(64 * (t % 4), 64), :] = tiles[t]

        def widen2(h):
            for w in range(n_plane):
                row = w * chunk2
                values = gath2[h, w].astype(F32)
                while row < min((w + 1) * chunk2, 864):
                    stop = min((row // 96 + 1) * 96, (w + 1) * chunk2, 864)
                    start = pl.multiple_of(row // 96 * 192 + row % 96 + h * 96, 8)
                    g2_out[pl.ds(start, stop - row), :] = values[row - w * chunk2 : stop - w * chunk2]
                    row = stop

        sum1[0][0].start()
        for copy in field_copies + hidden_copies + delta_copies:
            copy.wait_send()
        sum1[1]()
        sum2[2]()
        sum1[6]("first")
        sum2[6]("first", "spread")
        sum1[2]()
        sum1[6]("spread")
        sum2[3]()
        sum2[6]("around")
        sum1[3]()
        sum1[6]("around")
        sum2[4]()
        widen2(core)
        sum2[6]("back")
        sum1[4]()
        sum2[5]()
        sum2[6]("onward")
        widen2(1 - core)

        def widen(h):
            start = pl.multiple_of(h * (ROWS1 // 2), 8)
            full1[pl.ds(start, ROWS1 // 2), :] = gath1[h].astype(F32).reshape(ROWS1 // 2, 128)

        widen(core)
        sum1[6]("back")
        sum1[5]()
        widen(1 - core)
        for t in range(6):
            g1_out[:, pl.ds(128 * t, 128)] = full1[pl.ds(64 * t, 64), :]
        g1_out[:, pl.ds(768, 96)] = full1[pl.ds(384, 64), pl.ds(0, 96)]
        sum1[6]("onward")

    return kernel


def write_out(g1_in, g2_in, g1_out, g2_out, sems):
    second = pltpu.make_async_copy(g2_in, g2_out, sems.at[1])
    second.start()
    first = pltpu.make_async_copy(g1_in, g1_out, sems.at[0])
    first.start()
    first.wait()
    second.wait()


def solution(mesh):
    n_dep, n_row, n_col = mesh.shape["depth"], mesh.shape["row"], mesh.shape["col"]
    n_plane = n_dep * n_row // 2
    kernel = make_kernel(n_dep, n_row, n_col)
    n_sum = 3 * n_plane + n_col + 3

    def vm(shape, dtype):
        return pltpu.VMEM(shape, dtype)

    def sum_scratch(rows):
        half, chunk = rows // 2, rows // (2 * n_plane)
        return [
            vm((2, half, 128), F32), vm((half, 128), F32),
            vm((n_plane, chunk, 128), BF16), vm((n_plane, chunk, 128), BF16),
            vm((n_col, chunk, 128), BF16), vm((2, n_plane, chunk, 128), BF16),
        ]

    def shards(volume, first_weight, second_weight, cotangent):
        first_grad, second_grad = pl.pallas_call(
            kernel,
            out_shape=(
                jax.ShapeDtypeStruct((64, 864), F32),
                jax.ShapeDtypeStruct((1728, 128), F32),
            ),
            in_specs=[pl.BlockSpec(memory_space=pltpu.HBM)] * 4,
            out_specs=(pl.BlockSpec(memory_space=pltpu.VMEM),) * 2,
            scratch_shapes=[
                vm((8, 4, 16, 1024), BF16), vm((64, 864), BF16), vm((1728, 128), BF16), vm((8, 4, 1024), BF16),
                pltpu.SemaphoreType.DMA((4,)),
                vm((4, 9, 168, 128), F32), vm((5, 5, 9, 32, 128), BF16),
                vm((64, 896), F32), vm((9, 128, 256), BF16), vm((9, 256, 128), BF16), vm((8, 32, 128), F32),
                vm((128, 128), BF16), vm((8, 32, 128), BF16), vm((8, 128), F32),
                vm((128, 128), BF16), vm((9, 32, 128), BF16), vm((16, 1024), BF16), vm((16, 128), BF16),
                vm((8, 128), F32), vm((16, 128), BF16),
                vm((2, 2, 9, 48, 128), F32), vm((9, 9, 32, 128), BF16), vm((2, 2, 256, 128), F32),
                vm((4, 32, 128), BF16), vm((8, 16, 128), BF16), vm((4, 16, 128), BF16), vm((8, 128), F32),
                vm((4, 32, 128), BF16), vm((9, 16, 128), BF16), vm((4, 16, 128), BF16), vm((16, 128), BF16),
                vm((8, 128), F32), vm((8, 128), F32),
                vm((9, 40, 128), F32), vm((4, 9, 32, 128), BF16), vm((9, 128, 256), F32),
                vm((32, 128), BF16), vm((4, 16, 128), BF16), vm((4, 16, 128), BF16), vm((8, 128), F32),
                vm((32, 128), BF16), vm((4, 16, 128), BF16), vm((16, 128), BF16),
                vm((4, 16, 128), BF16), vm((16, 128), BF16), vm((8, 128), F32), vm((16, 128), BF16),
                *sum_scratch(ROWS1), vm((ROWS1, 128), F32), *sum_scratch(ROWS2),
                pltpu.SemaphoreType.DMA((24,)), pltpu.SemaphoreType.DMA((24,)),
                pltpu.SemaphoreType.DMA((n_sum,)), pltpu.SemaphoreType.DMA((n_sum,)),
                pltpu.SemaphoreType.DMA((n_sum,)), pltpu.SemaphoreType.DMA((n_sum,)),
            ],
            compiler_params=pltpu.CompilerParams(
                collective_id=0, has_side_effects=True, vmem_limit_bytes=48 * 1024 * 1024
            ),
            name="sections",
        )(*[
            pltpu.with_memory_space_constraint(x, pltpu.HBM)
            for x in (volume.reshape(8, 4, 16, 1024), first_weight, second_weight.T, cotangent)
        ])
        first_grad, second_grad = pl.pallas_call(
            write_out,
            out_shape=(
                jax.ShapeDtypeStruct((64, 864), F32),
                jax.ShapeDtypeStruct((1728, 128), F32),
            ),
            in_specs=[pl.BlockSpec(memory_space=pltpu.VMEM)] * 2,
            out_specs=(pl.BlockSpec(memory_space=pltpu.HBM),) * 2,
            scratch_shapes=[pltpu.SemaphoreType.DMA((2,))],
            name="write_out",
        )(pltpu.with_memory_space_constraint(first_grad, pltpu.VMEM), pltpu.with_memory_space_constraint(second_grad, pltpu.VMEM))
        return first_grad, second_grad.T

    placed = (P("depth", "row", "col"), P(), P(), P("depth", "row", "col"))
    return jax.shard_map(shards, mesh=mesh, in_specs=placed, out_specs=(P(), P()), check_vma=False)
```

```python
import jax
import jax.numpy as jnp
from jax import lax
from jax.experimental import pallas as pl
from jax.experimental.pallas import tpu as pltpu
from jax.sharding import PartitionSpec as P

MESH = pl.DeviceIdType.MESH
F32 = jnp.float32
BF16 = jnp.bfloat16

ROWS1, ROWS2 = 512, 1792


def leaky(values):
    root = lax.rsqrt(values * values + 1.0)
    return 0.6 * values + 0.4 * ((values * values + 1.0) * root - 1.0)


def leaky_slope(values):
    return 0.6 + 0.4 * values * lax.rsqrt(values * values + 1.0)


def dot_nt(lhs, rhs):
    return lax.dot_general(lhs, rhs, (((1,), (1,)), ((), ())), preferred_element_type=F32)


def dot_tn(lhs, rhs):
    return lax.dot_general(lhs, rhs, (((0,), (0,)), ((), ())), preferred_element_type=F32)


def dot_nn(lhs, rhs):
    return lax.dot_general(lhs, rhs, (((1,), (0,)), ((), ())), preferred_element_type=F32)


def window(ref, *lead):
    low = ref[lead + (pl.ds(0, 8),)].reshape(256, 128)
    high = ref[lead + (pl.ds(1, 8),)].reshape(256, 128)
    return jnp.concatenate([low, high], axis=1)


def make_kernel(n_dep, n_row, n_col):
    n_half = n_row // 2
    n_plane = n_dep * n_half

    def kernel(
        vol_in, w1_in, w2_in, cot_in, g1_out, g2_out,
        vol, w1, w2, cot, load_sem,
        s_ref, f_ref, w1f, w1b, w2b, up,
        f_sc, f_sr, f_sk, f_c, f_r, f_d, f_dc, f_dr, f_drc,
        hs, hx, slope1, h_sc, h_sr, h_sd, h_sk, h_c, h_r, h_d, h_dc, h_dr, h_drc,
        q_ref, dx, g1acc, q_sc, q_sr, q_sd, q_sk, q_c, q_r, q_rc, q_d, q_dc, q_dr, q_drc,
        acc1, swap1, send1, come1, cols1, gath1, full1,
        acc2, swap2, send2, come2, cols2, gath2,
        halo_send, halo_recv, sum_send1, sum_recv1, sum_send2, sum_recv2,
    ):
        dep, row, col = lax.axis_index("depth"), lax.axis_index("row"), lax.axis_index("col")
        core, line = lax.rem(row, 2), lax.div(row, 2)
        plane = dep * n_half + line

        loads = [
            pltpu.make_async_copy(src, dst, load_sem.at[i])
            for i, (src, dst) in enumerate(((vol_in, vol), (w1_in, w1), (w2_in, w2), (cot_in, cot)))
        ]
        loads[0].start()

        def plane_dev(index):
            return (lax.div(index, n_half), 2 * lax.rem(index, n_half) + core, col)

        def shifted(step, d, r, c):
            return (
                lax.rem(dep + d * step + n_dep, n_dep),
                lax.rem(row + r * step + n_row, n_row),
                lax.rem(col + c * step + n_col, n_col),
            )

        mate = (dep, row + 1 - 2 * core, col)
        corners = [(d, r, c) for d in (0, 1) for r in (0, 1) for c in (0, 1)][1:]

        barrier = pltpu.get_barrier_semaphore()
        peers = [shifted(s, *e) for e in corners for s in (1, -1)]
        peers.append(mate)
        peers += [plane_dev(lax.rem(plane + s, n_plane)) for s in range(1, n_plane)]
        peers += [(dep, row, lax.rem(col + s, n_col)) for s in range(1, n_col)]
        for peer in peers:
            pl.semaphore_signal(barrier, inc=1, device_id=peer, device_id_type=MESH)
        for load in loads[1:]:
            load.start()

        loads[0].wait()
        for rd in range(4):
            for t in (7, 0, 1, 2, 3, 4, 5, 6):
                s_ref[rd, 1 + t, pl.ds(24, 128), :] = (
                    vol[:, rd, :, pl.ds(128 * t, 128)].astype(F32).reshape(128, 128)
                )
        for t in range(8):
            rows = [s_ref[rd, 1 + t, pl.ds(24 + 15, 8, stride=16), :] for rd in range(4)]
            f_sr[t] = jnp.concatenate(rows, axis=0).astype(BF16)
        lane = lax.broadcasted_iota(jnp.int32, (128, 128), 1)
        packed = s_ref[3, 8, pl.ds(24, 128), :]
        for rd in range(3):
            moved = pltpu.roll(s_ref[rd, 8, pl.ds(24, 128), :], 32 * rd + 32, 1)
            packed = jnp.where((lane >= 32 * rd) & (lane < 32 * rd + 32), moved, packed)
        f_sc[...] = packed.astype(BF16)
        for t in range(8):
            f_sk[pl.ds(t, 1), :] = s_ref[3, 1 + t, pl.ds(151, 1), :]

        pl.semaphore_wait(barrier, len(peers))

        def halo(phase, kind, src, dst, step, index=None):
            index = phase * 7 + kind if index is None else index
            return pltpu.make_async_remote_copy(
                src_ref=src, dst_ref=dst, send_sem=halo_send.at[index], recv_sem=halo_recv.at[index],
                device_id=shifted(step, *corners[kind]), device_id_type=MESH,
            )

        field_copies = [
            halo(0, 6, f_sc.at[pl.ds(112, 16)], f_drc, 1),
            halo(0, 5, f_sk, f_dr, 1),
            halo(0, 4, f_sc.at[pl.ds(112, 16)], f_dc, 1),
            halo(0, 3, vol.at[7, 3], f_d, 1),
            halo(0, 2, f_sr.at[7], f_r.at[0], 1),
            halo(0, 1, f_sr, f_r.at[pl.ds(1, 8)], 1),
            halo(0, 0, f_sc, f_c, 1),
        ]
        for copy in field_copies:
            copy.start()

        for load in loads[1:]:
            load.wait()
        w1f[:, pl.ds(768, 128)] = jnp.zeros((64, 128), F32)
        w1f[:, pl.ds(0, 864)] = w1[...].astype(F32)
        lane1 = lax.broadcasted_iota(jnp.int32, (64, 256), 1)
        for ab in range(9):
            tile, off = divmod(ab * 96, 128)
            if tile == 6:
                band = jnp.concatenate([w1f[:, pl.ds(768, 128)], jnp.zeros((64, 128), F32)], axis=1)
            else:
                band = w1f[:, pl.ds(128 * tile, 256)]
            for kk, start in ((0, 96), (1, 160)):
                moved = pltpu.roll(band, (start - off) % 256, 1)
                keep = (lane1 >= start) & (lane1 < start + 96)
                w1b[ab, pl.ds(64 * kk, 64), :] = jnp.where(keep, moved, 0.0).astype(BF16)
            w2b[ab, pl.ds(0, 64), :] = jnp.zeros((64, 128), BF16)
            w2b[ab, pl.ds(64, 192), :] = w2[pl.ds(192 * ab, 192), :]
        for i in range(8):
            line_up = cot[i].astype(F32)
            for k in range(8):
                up[k, pl.ds(4 * i, 4), :] = line_up[:, 128 * k : 128 * (k + 1)]

        def pick_field(t, rd, rr):
            source, start = (3, 8) if rd < 0 else (rd, 24)
            rows = s_ref[source, t, pl.ds(start + rr, 32, stride=4), :]
            f_ref[rd + 1, rr + 1, t] = rows.astype(BF16)

        def local_tile(t, carry):
            for rd in range(4):
                for rr in range(4):
                    pick_field(t, rd, rr)
            return carry

        lax.fori_loop(1, 9, local_tile, 0)

        for rd in range(4):
            for rr in range(4):
                f_ref[rd + 1, rr + 1, 0] = jnp.zeros((32, 128), BF16)

        def tap_places(pd, pr, local):
            for ab in range(9):
                place = (2 * pd + ab // 3, 2 * pr + ab % 3)
                if (min(place) > 0) == local:
                    yield ab, place

        for pd in range(2):
            for pr in range(2):
                pre = jnp.zeros((256, 128), F32)
                for ab, place in tap_places(pd, pr, True):
                    pre += dot_nt(window(f_ref, *place), w1b[ab])
                slope1[pd, pr] = pre

        first_dep, first_row, first_col = dep == 0, row == 0, col == 0

        def unless(edge, values):
            return jnp.where(edge, 0.0, values.astype(F32))

        def first_section(pd, pr):
            edge = jnp.zeros((32, 128), F32)
            for ab, place in tap_places(pd, pr, True):
                edge += dot_nt(f_ref[place + (0,)], w1b[ab, :, pl.ds(0, 128)])
            pre = slope1[pd, pr]
            pre = jnp.concatenate([pre[:32] + edge, pre[32:]], axis=0)
            for ab, place in tap_places(pd, pr, False):
                pre += dot_nt(window(f_ref, *place), w1b[ab])
            hid = leaky(pre).reshape(8, 32, 128)
            hs[pd, pr, pl.ds(1, 8), pl.ds(8, 32), :] = hid
            slope1[pd, pr] = leaky_slope(pre)
            h_sc[2 * pd + pr] = hid[7].astype(BF16)

        hidden_copies = [
            halo(1, 6, h_sk, h_drc, 1),
            halo(1, 5, h_sk, h_dr, 1),
            halo(1, 1, h_sr, h_r.at[pl.ds(1, 8)], 1),
            halo(1, 2, h_sr.at[7], h_r.at[0], 1),
            halo(1, 3, h_sd, h_d, 1),
            halo(1, 4, h_sd.at[3], h_dc, 1),
            halo(1, 0, h_sc.at[3], h_c.at[3], 1),
            halo(1, 0, h_sc.at[1], h_c.at[1], 1, 21),
            halo(1, 0, h_sc.at[2], h_c.at[2], 1, 22),
            halo(1, 0, h_sc.at[0], h_c.at[0], 1, 23),
        ]
        field_copies[6].wait_recv()
        packed = unless(first_col, f_c[...])
        for rd in range(4):
            s_ref[rd, 0, pl.ds(24, 128), :] = packed if rd == 3 else pltpu.roll(packed, 96 - 32 * rd, 1)
        for rd in range(4):
            for rr in range(4):
                pick_field(0, rd, rr)
        first_section(1, 1)
        for t in range(8):
            h_sk[pl.ds(t, 1), :] = hs[1, 1, 1 + t, pl.ds(39, 1), :]
        for copy in hidden_copies[:2] + hidden_copies[6:7]:
            copy.start()

        field_copies[2].wait_recv()
        field_copies[3].wait_recv()
        for t in range(8):
            s_ref[3, 1 + t, pl.ds(8, 16), :] = unless(first_dep, f_d[:, pl.ds(128 * t, 128)])
        s_ref[3, 0, pl.ds(8, 16), :] = unless(first_dep | first_col, f_dc[...])

        def above_tile(t, carry):
            for rr in range(4):
                pick_field(t, -1, rr)
            return carry

        lax.fori_loop(0, 9, above_tile, 0)
        first_section(0, 1)
        for t in range(8):
            rows = [hs[pd, 1, 1 + t, pl.ds(11, 8, stride=4), :] for pd in range(2)]
            h_sr[t] = jnp.concatenate(rows, axis=0).astype(BF16)
        for copy in hidden_copies[2:4] + hidden_copies[7:8]:
            copy.start()

        field_copies[4].wait_recv()
        field_copies[5].wait_recv()

        def row_tile(t, carry):
            block = unless(first_row | (first_col & (t == 0)), f_r[t])
            for rd in range(4):
                s_ref[rd, t, pl.ds(23, 8, stride=16), :] = block[8 * rd : 8 * rd + 8]
            for rd in range(4):
                pick_field(t, rd, -1)
            return carry

        lax.fori_loop(0, 9, row_tile, 0)
        first_section(1, 0)
        for t in range(4):
            rows = [hs[1, pr, 1 + 2 * t + u, pl.ds(36, 4), :] for u in range(2) for pr in range(2)]
            h_sd[t] = jnp.concatenate(rows, axis=0).astype(BF16)
        for copy in hidden_copies[4:6] + hidden_copies[8:9]:
            copy.start()

        field_copies[0].wait_recv()
        field_copies[1].wait_recv()
        s_ref[3, 0, pl.ds(7, 1), :] = unless(first_dep | first_row | first_col, f_drc[...])[15:16]
        block = unless(first_dep | first_row, f_dr[...])
        for t in range(8):
            s_ref[3, 1 + t, pl.ds(7, 1), :] = block[t : t + 1]

        def edge_tile(t, carry):
            pick_field(t, -1, -1)
            return carry

        lax.fori_loop(0, 9, edge_tile, 0)
        first_section(0, 0)
        hidden_copies[9].start()

        def pick_hidden(a, b, pd, pr, start):
            hx[3 * a + b] = hs[pd, pr, :, pl.ds(start, 32), :].astype(BF16)

        for copy in hidden_copies:
            copy.wait_recv()
        for pd in range(2):
            for pr in range(2):
                hs[pd, pr, 0, pl.ds(8, 32), :] = unless(first_col, h_c[2 * pd + pr])
        for t in range(4):
            block = unless(first_dep, h_d[t])
            for u in range(2):
                for pr in range(2):
                    start = 8 * u + 4 * pr
                    hs[1, pr, 1 + 2 * t + u, pl.ds(4, 4), :] = block[start : start + 4]
        block = unless(first_dep | first_col, h_dc[...])
        for pr in range(2):
            hs[1, pr, 0, pl.ds(4, 4), :] = block[8 + 4 * pr : 12 + 4 * pr]
        for pr in range(2):
            pick_hidden(0, 1 + pr, 1, pr, 4)
            pick_hidden(1, 1 + pr, 0, pr, 8)
            pick_hidden(2, 1 + pr, 1, pr, 8)
        for t in range(9):
            edge = first_row | first_col if t == 0 else first_row
            block = unless(edge, h_r[t])
            for pd in range(2):
                hs[pd, 1, t, pl.ds(7, 8, stride=4), :] = block[8 * pd : 8 * pd + 8]
        block = unless(first_dep | first_row, h_dr[...])
        for t in range(8):
            hs[1, 1, 1 + t, pl.ds(3, 1), :] = block[t : t + 1]
        hs[1, 1, 0, pl.ds(3, 1), :] = unless(first_dep | first_row | first_col, h_drc[...])[7:8]
        pick_hidden(0, 0, 1, 1, 3)
        pick_hidden(1, 0, 0, 1, 7)
        pick_hidden(2, 0, 1, 1, 7)

        pre = jnp.zeros((256, 128), F32)
        for ab in range(9):
            pre += dot_nn(window(hx, ab), w2b[ab])
        delta2 = up[...].reshape(256, 128) * leaky_slope(pre)
        q_ref[pl.ds(0, 8), pl.ds(0, 32), :] = delta2.reshape(8, 32, 128)
        q_sc[...] = delta2[:32].astype(BF16)
        for t in range(4):
            rows = [q_ref[2 * t + u, pl.ds(0, 8, stride=4), :] for u in range(2)]
            q_sr[t] = jnp.concatenate(rows, axis=0).astype(BF16)
            rows = [q_ref[2 * t + u, pl.ds(0, 8), :] for u in range(2)]
            q_sd[t] = jnp.concatenate(rows, axis=0).astype(BF16)
        for t in range(8):
            q_sk[pl.ds(t, 1), :] = q_ref[t, pl.ds(0, 1), :]
        delta_copies = [
            halo(2, 6, q_sd.at[0], q_drc, -1),
            halo(2, 5, q_sk, q_dr, -1),
            halo(2, 4, q_sd.at[0], q_dc, -1),
            halo(2, 3, q_sd, q_d, -1),
            halo(2, 2, q_sr.at[0], q_rc, -1),
            halo(2, 1, q_sr, q_r, -1),
            halo(2, 0, q_sc, q_c, -1),
        ]
        for copy in reversed(delta_copies):
            copy.start()

        def summing(rows, acc, swap, send, come, cols, gath, sems_out, sems_in, cuts):
            half, chunk = rows // 2, rows // (2 * n_plane)

            def remote(index, src, dst, dev):
                return pltpu.make_async_remote_copy(
                    src_ref=src, dst_ref=dst, send_sem=sems_out.at[index], recv_sem=sems_in.at[index],
                    device_id=dev, device_id_type=MESH,
                )

            order = sorted(range(1, n_plane), key=lambda s: -min(s % n_half, n_half - s % n_half))
            pieces = [(low, high) for low, high in zip((0,) + cuts, cuts + (n_plane,)) if high > low]
            first = []
            for i, (low, high) in enumerate(pieces):
                part = pl.ds(low * chunk, (high - low) * chunk)
                first.append(remote(3 * n_plane + n_col + i, acc.at[1 - core, part], swap.at[part], mate))
            spread, around, back, onward = {}, {}, {}, {}
            own = gath.at[core, plane]
            for s in order:
                target = lax.rem(plane + s, n_plane)
                spread[s] = remote(s, send.at[target], come.at[s], plane_dev(target))
                back[s] = remote(n_plane + s, own, own, plane_dev(target))
                came = gath.at[core, lax.rem(plane - s + n_plane, n_plane)]
                onward[s] = remote(2 * n_plane + s, came, came, mate)
            onward[0] = remote(2 * n_plane, own, own, mate)
            for s in range(1, n_col):
                target = lax.rem(col + s, n_col)
                around[s] = remote(3 * n_plane + s, cols.at[col], cols.at[col], (dep, row, target))

            def to_plane():
                for (low, high), copy in zip(pieces, first):
                    copy.wait_recv()
                    part = pl.ds(low * chunk, (high - low) * chunk)
                    summed = acc[core, part, :] + swap[part, :]
                    send[pl.ds(low, high - low)] = summed.reshape(high - low, chunk, 128).astype(BF16)
                for s in order:
                    spread[s].start()

            def to_column():
                place = pl.multiple_of(plane * chunk, 8)
                total = acc[core, pl.ds(place, chunk), :] + swap[pl.ds(place, chunk), :]
                for s in reversed(order):
                    spread[s].wait_recv()
                    total += come[s].astype(F32)
                cols[col] = total.astype(BF16)
                for s in sorted(around, key=lambda s: -min(s, n_col - s)):
                    around[s].start()

            def to_all():
                for s in around:
                    around[s].wait_recv()
                total = cols[0].astype(F32)
                for k in range(1, n_col):
                    total += cols[k].astype(F32)
                gath[core, plane] = total.astype(BF16)
                for s in order:
                    back[s].start()
                onward[0].start()

            def to_mate():
                for s in reversed(order):
                    back[s].wait_recv()
                    onward[s].start()

            def finish():
                for s in onward:
                    onward[s].wait_recv()

            def drain(*names):
                for name in names:
                    group = {"first": dict(enumerate(first)), "spread": spread, "around": around, "back": back, "onward": onward}[name]
                    for s in group:
                        group[s].wait_send()

            return list(first), to_plane, to_column, to_all, to_mate, finish, drain

        sum1 = summing(ROWS1, acc1, swap1, send1, come1, cols1, gath1, sum_send1, sum_recv1, ())
        chunk2 = ROWS2 // (2 * n_plane)
        sum2 = summing(ROWS2, acc2, swap2, send2, come2, cols2, gath2, sum_send2, sum_recv2, (288 // chunk2, 576 // chunk2))

        flat2 = delta2.astype(BF16)
        acc2[:, pl.ds(864, 32), :] = jnp.zeros((2, 32, 128), F32)
        ready = 0
        for ab in range(9):
            grad = dot_tn(window(hx, ab), flat2)
            for h in range(2):
                acc2[h, pl.ds(96 * ab, 96), :] = grad[64 + 96 * h : 160 + 96 * h]
            if ab % 3 == 2:
                whole = n_plane if ab == 8 else 96 * (ab + 1) // chunk2
                if whole > ready:
                    sum2[0].pop(0).start()
                ready = whole
        sum2[1]()

        last_dep, last_row, last_col = dep == n_dep - 1, row == n_row - 1, col == n_col - 1
        taps = (((1, 0),), ((2, 0), (0, 1)))

        def way_back(pd, pr):
            back = jnp.zeros((256, 128), F32)
            for a, od in taps[pd]:
                for b, o_r in taps[pr]:
                    band = jnp.concatenate(
                        [w2b[3 * a + b, pl.ds(128, 128), :], w2b[3 * a + b, pl.ds(0, 128), :]], axis=1
                    )
                    back += dot_nt(window(dx, 2 * od + o_r), band)
            delta1 = (back * slope1[pd, pr]).T.astype(BF16)
            for ab in range(9):
                a, b = divmod(ab, 3)
                grad = dot_nn(delta1, window(f_ref, 2 * pd + a, 2 * pr + b))
                if pd + pr > 0:
                    grad += g1acc[ab]
                if pd + pr < 2:
                    g1acc[ab] = grad
                else:
                    yield grad

        delta_copies[6].wait_recv()
        q_ref[8, pl.ds(0, 32), :] = unless(last_col, q_c[...])
        dx[0] = q_ref[:, pl.ds(0, 32), :].astype(BF16)
        list(way_back(0, 0))
        delta_copies[2].wait_recv()
        delta_copies[3].wait_recv()
        for t in range(8):
            u = 8 * (t % 2)
            q_ref[t, pl.ds(32, 4), :] = unless(last_dep, q_d[t // 2])[u : u + 4]
        q_ref[8, pl.ds(32, 4), :] = unless(last_dep | last_col, q_dc[...])[:4]
        dx[2] = q_ref[:, pl.ds(4, 32), :].astype(BF16)
        list(way_back(1, 0))
        delta_copies[4].wait_recv()
        delta_copies[5].wait_recv()
        for t in range(8):
            u = 8 * (t % 2)
            q_ref[t, pl.ds(4, 8, stride=4), :] = unless(last_row, q_r[t // 2])[u : u + 8]
        q_ref[8, pl.ds(4, 8, stride=4), :] = unless(last_row | last_col, q_rc[...])[:8]
        dx[1] = q_ref[:, pl.ds(1, 32), :].astype(BF16)
        list(way_back(0, 1))
        delta_copies[0].wait_recv()
        delta_copies[1].wait_recv()
        block = unless(last_dep | last_row, q_dr[...])
        for t in range(8):
            q_ref[t, pl.ds(36, 1), :] = block[t : t + 1]
        q_ref[8, pl.ds(36, 1), :] = unless(last_dep | last_row | last_col, q_drc[...])[:1]
        dx[3] = q_ref[:, pl.ds(5, 32), :].astype(BF16)

        lane = lax.broadcasted_iota(jnp.int32, (64, 256), 1)
        tiles = [jnp.zeros((64, 128), F32) for _ in range(8)]
        for ab, grad in enumerate(way_back(1, 1)):
            both = grad[:64] + pltpu.roll(grad[64:], 256 - 64, 1)
            both = jnp.where((lane >= 96) & (lane < 192), both, 0.0)
            tile, off = divmod(ab * 96, 128)
            both = pltpu.roll(both, (off - 96) % 256, 1)
            tiles[tile] = tiles[tile] + both[:, :128]
            tiles[tile + 1] = tiles[tile + 1] + both[:, 128:]
        for t in range(8):
            acc1[t // 4, pl.ds(64 * (t % 4), 64), :] = tiles[t]

        def widen2(h):
            for w in range(n_plane):
                row = w * chunk2
                values = gath2[h, w].astype(F32)
                while row < min((w + 1) * chunk2, 864):
                    stop = min((row // 96 + 1) * 96, (w + 1) * chunk2, 864)
                    start = pl.multiple_of(row // 96 * 192 + row % 96 + h * 96, 8)
                    g2_out[pl.ds(start, stop - row), :] = values[row - w * chunk2 : stop - w * chunk2]
                    row = stop

        sum1[0][0].start()
        for copy in field_copies + hidden_copies + delta_copies:
            copy.wait_send()
        sum1[1]()
        sum2[2]()
        sum1[6]("first")
        sum2[6]("first", "spread")
        sum1[2]()
        sum1[6]("spread")
        sum2[3]()
        sum2[6]("around")
        sum1[3]()
        sum1[6]("around")
        sum2[4]()
        sum1[4]()
        widen2(core)
        sum2[6]("back")
        sum2[5]()
        sum2[6]("onward")
        widen2(1 - core)

        def widen(h):
            start = pl.multiple_of(h * (ROWS1 // 2), 8)
            full1[pl.ds(start, ROWS1 // 2), :] = gath1[h].astype(F32).reshape(ROWS1 // 2, 128)

        widen(core)
        sum1[6]("back")
        sum1[5]()
        widen(1 - core)
        for t in range(6):
            g1_out[:, pl.ds(128 * t, 128)] = full1[pl.ds(64 * t, 64), :]
        g1_out[:, pl.ds(768, 96)] = full1[pl.ds(384, 64), pl.ds(0, 96)]
        sum1[6]("onward")

    return kernel


def write_out(g1_in, g2_in, g1_out, g2_out, sems):
    second = pltpu.make_async_copy(g2_in, g2_out, sems.at[1])
    second.start()
    first = pltpu.make_async_copy(g1_in, g1_out, sems.at[0])
    first.start()
    first.wait()
    second.wait()


def solution(mesh):
    n_dep, n_row, n_col = mesh.shape["depth"], mesh.shape["row"], mesh.shape["col"]
    n_plane = n_dep * n_row // 2
    kernel = make_kernel(n_dep, n_row, n_col)
    n_sum = 3 * n_plane + n_col + 3

    def vm(shape, dtype):
        return pltpu.VMEM(shape, dtype)

    def sum_scratch(rows):
        half, chunk = rows // 2, rows // (2 * n_plane)
        return [
            vm((2, half, 128), F32), vm((half, 128), F32),
            vm((n_plane, chunk, 128), BF16), vm((n_plane, chunk, 128), BF16),
            vm((n_col, chunk, 128), BF16), vm((2, n_plane, chunk, 128), BF16),
        ]

    def shards(volume, first_weight, second_weight, cotangent):
        first_grad, second_grad = pl.pallas_call(
            kernel,
            out_shape=(
                jax.ShapeDtypeStruct((64, 864), F32),
                jax.ShapeDtypeStruct((1728, 128), F32),
            ),
            in_specs=[pl.BlockSpec(memory_space=pltpu.HBM)] * 4,
            out_specs=(pl.BlockSpec(memory_space=pltpu.VMEM),) * 2,
            scratch_shapes=[
                vm((8, 4, 16, 1024), BF16), vm((64, 864), BF16), vm((1728, 128), BF16), vm((8, 4, 1024), BF16),
                pltpu.SemaphoreType.DMA((4,)),
                vm((4, 9, 168, 128), F32), vm((5, 5, 9, 32, 128), BF16),
                vm((64, 896), F32), vm((9, 128, 256), BF16), vm((9, 256, 128), BF16), vm((8, 32, 128), F32),
                vm((128, 128), BF16), vm((8, 32, 128), BF16), vm((8, 128), F32),
                vm((128, 128), BF16), vm((9, 32, 128), BF16), vm((16, 1024), BF16), vm((16, 128), BF16),
                vm((8, 128), F32), vm((16, 128), BF16),
                vm((2, 2, 9, 48, 128), F32), vm((9, 9, 32, 128), BF16), vm((2, 2, 256, 128), F32),
                vm((4, 32, 128), BF16), vm((8, 16, 128), BF16), vm((4, 16, 128), BF16), vm((8, 128), F32),
                vm((4, 32, 128), BF16), vm((9, 16, 128), BF16), vm((4, 16, 128), BF16), vm((16, 128), BF16),
                vm((8, 128), F32), vm((8, 128), F32),
                vm((9, 40, 128), F32), vm((4, 9, 32, 128), BF16), vm((9, 128, 256), F32),
                vm((32, 128), BF16), vm((4, 16, 128), BF16), vm((4, 16, 128), BF16), vm((8, 128), F32),
                vm((32, 128), BF16), vm((4, 16, 128), BF16), vm((16, 128), BF16),
                vm((4, 16, 128), BF16), vm((16, 128), BF16), vm((8, 128), F32), vm((16, 128), BF16),
                *sum_scratch(ROWS1), vm((ROWS1, 128), F32), *sum_scratch(ROWS2),
                pltpu.SemaphoreType.DMA((24,)), pltpu.SemaphoreType.DMA((24,)),
                pltpu.SemaphoreType.DMA((n_sum,)), pltpu.SemaphoreType.DMA((n_sum,)),
                pltpu.SemaphoreType.DMA((n_sum,)), pltpu.SemaphoreType.DMA((n_sum,)),
            ],
            compiler_params=pltpu.CompilerParams(
                collective_id=0, has_side_effects=True, vmem_limit_bytes=48 * 1024 * 1024
            ),
            name="sections",
        )(*[
            pltpu.with_memory_space_constraint(x, pltpu.HBM)
            for x in (volume.reshape(8, 4, 16, 1024), first_weight, second_weight.T, cotangent)
        ])
        first_grad, second_grad = pl.pallas_call(
            write_out,
            out_shape=(
                jax.ShapeDtypeStruct((64, 864), F32),
                jax.ShapeDtypeStruct((1728, 128), F32),
            ),
            in_specs=[pl.BlockSpec(memory_space=pltpu.VMEM)] * 2,
            out_specs=(pl.BlockSpec(memory_space=pltpu.HBM),) * 2,
            scratch_shapes=[pltpu.SemaphoreType.DMA((2,))],
            name="write_out",
        )(pltpu.with_memory_space_constraint(first_grad, pltpu.VMEM), pltpu.with_memory_space_constraint(second_grad, pltpu.VMEM))
        return first_grad, second_grad.T

    placed = (P("depth", "row", "col"), P(), P(), P("depth", "row", "col"))
    return jax.shard_map(shards, mesh=mesh, in_specs=placed, out_specs=(P(), P()), check_vma=False)
```
